256 devices in a mesh: grp: 8 (over x, y_hi), vocab: 32 (over y_lo, z, core).
Axes of the slice: x: 4, y: 4 (y_hi: 2, y_lo: 2; y = y_hi * 2 + y_lo), z: 8, core: 2. Of those that a mesh axis runs over, the one named last changes fastest.
Arguments:
- hidden: bfloat16 [1024, 4096], P('grp'), may hold values from -360 to 360
- weight: bfloat16 [4096, 75968], P('grp', 'vocab'), may hold values from -0.09375 to 0.09375
- teacher_panels: bfloat16 [512, 151936], P('grp', 'vocab'), may hold values from -20 to 172
- token_ids: int32 [1024], P('grp'), may hold values from 0 to 75967
- row_counts: int32 [8], P('grp'), may hold values from 64 to 128, as said below
Outputs:
- row_kl: float32 [1024], P('grp')
- hidden_grad: bfloat16 [1024, 4096], P('grp', 'vocab')
- weight_grad: bfloat16 [4096, 75968], P('grp', 'vocab')
The draws below stay inside these ranges and needn't reach their ends.
Inputs may be any that keep to these rules, and one draw needn't show every extreme that they name: `row_counts`: one group's count is exactly 128.
All inputs are finite; a program needn't handle non-finite values.
Results may differ from the reference program's by a relative error of at most 0.005.
Values may be sent and summed in bfloat16 or wider, within the bound.
A program may use at most 128 MiB of HBM per device.

```python
import jax
import jax.numpy as jnp

D = 4096
V = 75968
KL_SCALE = 256
ROWS = 128
GROUPS = 8
TOKENS = 1024
VS = 2374
N_VOCAB = 32


def draw_hidden(key, part):
    key = jax.random.fold_in(key, 11)
    key_base = jax.random.fold_in(key, 0)
    values = jnp.clip(jax.random.normal(key_base, (TOKENS, D), jnp.float32), -6.0, 6.0)
    return values.astype(jnp.bfloat16)


def draw_teacher_panels(key, part):
    key = jax.random.fold_in(key, 23)
    key_base = jax.random.fold_in(key, 0)
    shape_rows = TOKENS // 2
    values = jnp.clip(3.0 * jax.random.normal(key_base, (shape_rows, 2 * V), jnp.float32), -18.0, 18.0)
    return values.astype(jnp.bfloat16)


def draw_row_counts(key, part):
    key = jax.random.fold_in(key, 37)
    key_base, key_full = jax.random.split(key)
    counts = jax.random.randint(key_base, (GROUPS,), ROWS // 2, ROWS + 1)
    full_group = jax.random.randint(key_full, (), 0, GROUPS)
    return jnp.where(jnp.arange(GROUPS, dtype=jnp.int32) == full_group, ROWS, counts).astype(jnp.int32)


def place_ends(entries, stream_key, least, high):
    dims = entries.shape
    place = [jax.random.randint(jax.random.fold_in(stream_key, axis), (), 0, dims[axis]) for axis in range(len(dims))]
    entries = entries.at[tuple(place)].set(least)
    longest = dims.index(max(dims))
    place[longest] = (place[longest] + 1) % dims[longest]
    return entries.at[tuple(place)].set(high)


def shard_levels(rng, shape, cuts, least, largest):
    gain = 1.0
    for position, shards_of in cuts:
        heights = jax.random.uniform(jax.random.fold_in(jax.random.fold_in(rng, 6), position), (shards_of,), jnp.float32, least / len(cuts), largest / len(cuts))
        gain = gain * jnp.repeat(jnp.exp(heights), shape[position] // shards_of).reshape((-1,) + (1,) * (len(shape) - 1 - position))
    return gain


def gaussian(stream_key, shape, deviation, limit, pieces=(), kind=jnp.bfloat16):
    level = shard_levels(stream_key, shape, pieces, -0.22, 0.18) if pieces else 1.0
    result = jax.random.normal(stream_key, shape, jnp.float32) * deviation * level
    return jnp.minimum(jnp.maximum(result, -limit), limit).astype(kind)


def setup_inputs(seed: int = 0) -> dict:
    seeds = jax.random.split(jax.random.key(seed), 6)
    hidden = draw_hidden(jax.random.fold_in(seeds[5], 71), 0)
    weight = gaussian(seeds[1], (D, V), D ** -0.5, 0.09375, ((0, 8), (1, 32)))
    teacher_panels = draw_teacher_panels(jax.random.fold_in(seeds[5], 71), 0)
    token_ids = place_ends(jax.random.randint(seeds[3], (TOKENS,), 0, V), jax.random.fold_in(seeds[3], 1), 0, V - 1).astype(jnp.int32)
    row_counts = draw_row_counts(jax.random.fold_in(seeds[5], 71), 0)
    return {"hidden": hidden, "weight": weight, "teacher_panels": teacher_panels, "token_ids": token_ids, "row_counts": row_counts}


def reference(hidden, weight, teacher_panels, token_ids, row_counts):
    panels = teacher_panels.astype(jnp.float32).reshape(GROUPS, ROWS // 2, N_VOCAB // 2, 2, 2 * VS)
    teacher = jnp.transpose(panels, (0, 3, 1, 2, 4)).reshape(TOKENS, V)
    logits = jnp.dot(hidden, weight, preferred_element_type=jnp.float32)
    peak_s = jnp.max(logits, axis=1)
    student_exp = jnp.exp(logits - peak_s[:, None])
    total_s = jnp.sum(student_exp, axis=1)
    student_norm = peak_s + jnp.log(total_s)
    peak_t = jnp.max(teacher, axis=1)
    total_t = jnp.sum(jnp.exp(teacher - peak_t[:, None]), axis=1)
    teacher_norm = peak_t + jnp.log(total_t)
    probs = student_exp / total_s[:, None]
    log_ratio = (logits - student_norm[:, None]) - (teacher - teacher_norm[:, None])
    divergence = jnp.sum(probs * log_ratio, axis=1)
    vocab_ids = jnp.arange(V, dtype=jnp.int32)
    chosen = (token_ids[:, None] == vocab_ids[None, :]).astype(jnp.float32)
    pick_student = jnp.sum(chosen * logits, axis=1)
    pick_teacher = jnp.sum(chosen * teacher, axis=1)
    advantage = (pick_teacher - teacher_norm) - (pick_student - student_norm)
    positions = jnp.arange(TOKENS, dtype=jnp.int32)
    limits = row_counts[positions // ROWS]
    valid = (positions % ROWS) < limits
    total_rows = jnp.sum(row_counts.astype(jnp.float32))
    row_weight = jnp.where(valid, ROWS / total_rows, jnp.zeros_like(total_rows))
    grad_logits = (row_weight[:, None] * (KL_SCALE * probs * (log_ratio - divergence[:, None]) - advantage[:, None] * (chosen - probs))).astype(jnp.bfloat16)
    row_kl = jnp.where(valid, divergence, jnp.zeros_like(divergence))
    hidden_grad = jnp.dot(grad_logits, weight.T, preferred_element_type=jnp.float32).astype(jnp.bfloat16)
    weight_grad = jnp.dot(hidden.T, grad_logits, preferred_element_type=jnp.float32).astype(jnp.bfloat16)
    return (row_kl, hidden_grad, weight_grad)
```

```python
import functools

import jax
import jax.numpy as jnp
from jax import lax
from jax.experimental import pallas as pl
from jax.experimental.pallas import tpu as pltpu
from jax.sharding import PartitionSpec as P

KL_SCALE = 256.0
MESH = pl.DeviceIdType.MESH
LOW = -1e30
NX, NH, NYL, NZ, NC = 4, 2, 2, 8, 2
TILE = 128
GROUP_PEERS = [(dx, dh) for dh in (1, 0) for dx in (1, 3, 2, 0) if dx or dh]
PAIR_PEERS = [(dx, dc) for dc in (0, 1) for dx in (1, 3, 2, 0) if dx or dc]
LINE_PEERS = [(dy, dz) for dy in (0, 1) for dz in range(NZ) if dy or dz]


def place():
    g = lax.axis_index("grp")
    v = lax.axis_index("vocab")
    return g // 2, g % 2, v // 16, (v // 2) % 8, v % 2


def device(x, h, yl, z, c):
    return {"grp": x * 2 + h, "vocab": yl * 16 + z * 2 + c}


def send(src, dst, ssem, rsem, target):
    copy = pltpu.make_async_remote_copy(
        src_ref=src, dst_ref=dst, send_sem=ssem, recv_sem=rsem, device_id=target, device_id_type=MESH
    )
    copy.start()
    return copy


def arrived(ref, sem):
    pltpu.make_async_copy(ref, ref, sem).wait()


def to_columns(tile):
    return jnp.transpose(jnp.concatenate([tile] * (TILE // 8), axis=0))


def merge(buf):
    peak_s = jnp.max(buf[:, :, 0], axis=0)
    scale_s = jnp.exp(buf[:, :, 0] - peak_s[None])
    peak_t = jnp.max(buf[:, :, 3], axis=0)
    scale_t = jnp.exp(buf[:, :, 3] - peak_t[None])
    return [
        peak_s,
        jnp.sum(buf[:, :, 1] * scale_s, axis=0),
        jnp.sum(buf[:, :, 2] * scale_s, axis=0),
        peak_t,
        jnp.sum(buf[:, :, 4] * scale_t, axis=0),
        jnp.sum(buf[:, :, 5], axis=0),
        jnp.sum(buf[:, :, 6], axis=0),
    ]


def loss_kernel(
    slab,
    chunks,
    hidden_ref,
    weight_ref,
    teacher_ref,
    meta_ref,
    grad_ref,
    own_ref,
    kl_ref,
    wide,
    heads,
    partial,
    landed,
    logits,
    teach,
    metas,
    near,
    far,
    outcome,
    cols,
    local_sem,
    hid_s,
    hid_r,
    fwd_s,
    fwd_r,
    core_s,
    core_r,
    meta_s,
    meta_r,
    w_s,
    w_r,
    half_s,
    half_r,
    t_s,
    t_r,
    near_s,
    near_r,
    far_s,
    far_r,
):
    x, h, yl, z, c = place()
    rows, depth = hidden_ref.shape[0], weight_ref.shape[0]
    half = NX * rows
    width = weight_ref.shape[1] // NX
    z_pair = z + 1 - 2 * lax.rem(z, 2)
    barrier = pltpu.get_barrier_semaphore()
    peers = [device((x + dx) % NX, (h + dh) % NH, yl, z, c) for dx, dh in GROUP_PEERS]
    peers += [device((x + dx) % NX, h, yl, z, 1 - c) for dx in range(NX)]
    peers += [device(x, h, (yl + dy) % NYL, (z + dz) % NZ, c) for dy, dz in LINE_PEERS]
    for peer in peers:
        pl.semaphore_signal(barrier, inc=1, device_id=peer, device_id_type=MESH)
    pl.semaphore_wait(barrier, len(peers))

    pending = []
    parity = lax.rem(z, 2)
    mine = 2 * c + parity

    def region(xs, hs, kx):
        return wide.at[
            pl.ds(pl.multiple_of(hs * half + xs * rows, rows), rows),
            pl.ds(pl.multiple_of(kx * depth, depth), depth),
        ]

    def block(kx, hs):
        return hidden_ref.at[:, pl.ds(pl.multiple_of((kx * 2 + hs) * depth, depth), depth)]

    for k, (dx, dh) in enumerate(GROUP_PEERS):
        xt, ht = (x + dx) % NX, (h + dh) % NH
        target = device(xt, ht, yl, z, c)
        pending.append(send(block(mine, ht), region(x, h, mine), hid_s.at[k], hid_r.at[k], target))
        pending.append(send(meta_ref, metas.at[x * 2 + h], meta_s.at[k], meta_r.at[k], target))
    for j, (low, size) in enumerate(chunks):
        for k, dx in enumerate((1, 3, 2)):
            xt = (x + dx) % NX
            pending.append(
                send(
                    weight_ref.at[:, pl.ds(pl.multiple_of(xt * width + low, TILE), size)],
                    heads.at[pl.ds(pl.multiple_of(x * depth, depth), depth), pl.ds(low, size)],
                    w_s.at[j * 3 + k],
                    w_r.at[j * 3 + k],
                    device(xt, h, yl, z, c),
                )
            )
    locals_ = []
    for kx in range(NX):
        locals_.append(pltpu.make_async_copy(block(kx, h), region(x, h, kx), local_sem.at[kx]))
    locals_.append(
        pltpu.make_async_copy(
            weight_ref.at[:, pl.ds(pl.multiple_of(x * width, TILE), width)],
            heads.at[pl.ds(pl.multiple_of(x * depth, depth), depth), :],
            local_sem.at[NX],
        )
    )
    locals_.append(
        pltpu.make_async_copy(
            teacher_ref.at[c, :, pl.ds(pl.multiple_of(x * width, TILE), width)],
            teach.at[pl.ds(pl.multiple_of(x * rows + c * (rows // 2), rows // 2), rows // 2), :],
            local_sem.at[NX + 1],
        )
    )
    for copy in locals_:
        copy.start()
    metas[x * 2 + h] = meta_ref[...]

    n = len(GROUP_PEERS)
    for k, (dx, dh) in enumerate(GROUP_PEERS):
        xs, hs = (x - dx + NX) % NX, (h + dh) % NH
        spot = region(xs, hs, mine)
        arrived(spot, hid_r.at[k])
        pending.append(send(spot, spot, fwd_s.at[k], fwd_r.at[k], device(x, h, yl, z_pair, c)))
        pending.append(send(spot, spot, core_s.at[k], core_r.at[k], device(x, h, yl, z, 1 - c)))
    for k, (dx, dh) in enumerate(GROUP_PEERS):
        xs, hs = (x - dx + NX) % NX, (h + dh) % NH
        spot = region(xs, hs, 2 * c + 1 - parity)
        arrived(spot, fwd_r.at[k])
        pending.append(send(spot, spot, core_s.at[n + k], core_r.at[n + k], device(x, h, yl, z, 1 - c)))
    for k, (dx, dh) in enumerate(GROUP_PEERS):
        xs, hs = (x - dx + NX) % NX, (h + dh) % NH
        arrived(region(xs, hs, 2 * (1 - c) + parity), core_r.at[k])
        arrived(region(xs, hs, 2 * (1 - c) + 1 - parity), core_r.at[n + k])
        arrived(metas.at[xs * 2 + hs], meta_r.at[k])
    for copy in locals_:
        copy.wait()

    def product(side, low, size):
        start = pl.multiple_of(side * half, half)
        return jnp.dot(
            wide[pl.ds(start, half), :], heads[:, low : low + size], preferred_element_type=jnp.float32
        )

    for j, (low, size) in enumerate(chunks):
        for k, dx in enumerate((1, 3, 2)):
            xs = (x - dx + NX) % NX
            arrived(
                heads.at[pl.ds(pl.multiple_of(xs * depth, depth), depth), pl.ds(low, size)],
                w_r.at[j * 3 + k],
            )
        if j == len(chunks) - 1:
            for k, (dx, dc) in enumerate(PAIR_PEERS):
                xt, ct = (x + dx) % NX, (c + dc) % NC
                pending.append(
                    send(
                        teacher_ref.at[ct, :, pl.ds(pl.multiple_of(xt * width, TILE), width)],
                        teach.at[pl.ds(pl.multiple_of(x * rows + c * (rows // 2), rows // 2), rows // 2), :],
                        t_s.at[k],
                        t_r.at[k],
                        device(xt, h, yl, z, ct),
                    )
                )
        partial[:, low : low + size] = product(1 - h, low, size)
        piece = pl.ds(low, size)
        pending.append(
            send(
                partial.at[:, piece], landed.at[:, piece], half_s.at[j], half_r.at[j],
                device(x, 1 - h, yl, z, c),
            )
        )
        logits[:, low : low + size] = product(h, low, size)
    own_ref[...] = wide[:, pl.ds(pl.multiple_of(x * depth, depth), depth)]
    for k, (dx, dc) in enumerate(PAIR_PEERS):
        xs, cs = (x - dx + NX) % NX, (c + dc) % NC
        arrived(
            teach.at[pl.ds(pl.multiple_of(xs * rows + cs * (rows // 2), rows // 2), rows // 2), :], t_r.at[k]
        )
    for j, (low, size) in enumerate(chunks):
        arrived(landed.at[:, pl.ds(low, size)], half_r.at[j])

    step = rows // 2
    lane = lax.broadcasted_iota(jnp.int32, (step, TILE), 1)
    column = lax.broadcasted_iota(jnp.int32, (step, width), 1)
    inside = column < slab - x * width
    base = ((yl * 16 + z * 2 + c) * slab + x * width).astype(jnp.float32)
    column_f = column.astype(jnp.float32)

    def fill(group, carry):
        cols[pl.ds(pl.multiple_of(group * rows, rows), rows), :] = to_columns(metas[group * 2 + h])
        return carry

    lax.fori_loop(0, NX, fill, 0)

    def measure(i, carry):
        span = pl.ds(pl.multiple_of(i * step, step), step)
        student = jnp.where(inside, logits[span, :] + landed[span, :], LOW)
        logits[span, :] = student
        raw = teach[span, :].astype(jnp.float32)
        teacher = jnp.where(inside, raw, LOW)
        chosen = (column_f == cols[span, :][:, 0:1] - base) & inside
        peak_s = jnp.max(student, axis=1, keepdims=True)
        peak_t = jnp.max(teacher, axis=1, keepdims=True)
        exp_s = jnp.exp(student - peak_s)
        exp_t = jnp.exp(teacher - peak_t)
        found = [
            peak_s,
            jnp.sum(exp_s, axis=1, keepdims=True),
            jnp.sum(exp_s * (student - raw), axis=1, keepdims=True),
            peak_t,
            jnp.sum(exp_t, axis=1, keepdims=True),
            jnp.sum(jnp.where(chosen, student, 0.0), axis=1, keepdims=True),
            jnp.sum(jnp.where(chosen, raw, 0.0), axis=1, keepdims=True),
        ]
        table = jnp.zeros((step, TILE), jnp.float32)
        for k, value in enumerate(found):
            table = jnp.where(lane == k + 1, value, table)
        cols[span, :] = jnp.where(lane == 0, cols[span, :], table)
        return carry

    lax.fori_loop(0, half // step, measure, 0)

    def pack(group, carry):
        table = jnp.transpose(cols[pl.ds(pl.multiple_of(group * rows, rows), rows), :])
        near[0, group] = table[0:8]
        return carry

    lax.fori_loop(0, NX, pack, 0)
    for k, (dx, dc) in enumerate(PAIR_PEERS):
        target = device((x + dx) % NX, h, yl, z, (c + dc) % NC)
        pending.append(send(near.at[0], near.at[k + 1], near_s.at[k], near_r.at[k], target))
    for k in range(len(PAIR_PEERS)):
        arrived(near.at[k + 1], near_r.at[k])

    merged = merge(near[:, :, 1:8])
    token_row = near[0, :, 0]
    for k, value in enumerate(merged):
        far[0, :, k] = value
    far[0, :, 7] = token_row
    for k, (dy, dz) in enumerate(LINE_PEERS):
        target = device(x, h, (yl + dy) % NYL, (z + dz) % NZ, c)
        pending.append(send(far.at[0], far.at[k + 1], far_s.at[k], far_r.at[k], target))
    for k in range(len(LINE_PEERS)):
        arrived(far.at[k + 1], far_r.at[k])
    peak_s, sum_s, weighted, peak_t, sum_t, pick_s, pick_t = merge(far[...])

    total_rows = jnp.sum(metas[:, 1, 0:1])
    student_norm = peak_s + jnp.log(sum_s)
    teacher_norm = peak_t + jnp.log(sum_t)
    mean_gap = weighted / sum_s
    divergence = mean_gap - student_norm + teacher_norm
    advantage = (pick_t - teacher_norm) - (pick_s - student_norm)
    counts = jnp.stack([metas[group * 2 + h][1] for group in range(NX)], axis=0)
    valid = lax.broadcasted_iota(jnp.int32, (NX, rows), 1).astype(jnp.float32) < counts
    row_weight = jnp.where(valid, rows / total_rows, 0.0)
    kl = jnp.where(valid, divergence, 0.0)
    own_group = lax.broadcasted_iota(jnp.int32, (NX, rows), 0) == x
    kl_ref[...] = jnp.sum(jnp.where(own_group, kl, 0.0), axis=0, keepdims=True)
    table = [
        peak_s, 1.0 / sum_s, mean_gap, row_weight * KL_SCALE, row_weight * advantage, token_row,
        token_row, token_row,
    ]
    for k, value in enumerate(table):
        outcome[:, k] = value

    def unpack(group, carry):
        cols[pl.ds(pl.multiple_of(group * rows, rows), rows), :] = to_columns(outcome[group])
        return carry

    lax.fori_loop(0, NX, unpack, 0)

    def finish(i, carry):
        span = pl.ds(pl.multiple_of(i * step, step), step)
        student = logits[span, :]
        raw = teach[span, :].astype(jnp.float32)
        table = cols[span, :]
        probs = jnp.exp(student - table[:, 0:1]) * table[:, 1:2]
        chosen = (column_f == table[:, 5:6] - base) & inside
        adv = table[:, 4:5]
        grad = probs * (table[:, 3:4] * ((student - raw) - table[:, 2:3]) + adv) - jnp.where(chosen, adv, 0.0)
        grad_ref[span, :] = grad.astype(jnp.bfloat16)
        return carry

    lax.fori_loop(0, half // step, finish, 0)
    for copy in pending:
        copy.wait_send()


def grads_kernel(
    grad_ref,
    own_ref,
    weight_ref,
    head_ref,
    hidden_ref,
    every,
    turned,
    rows_acc,
    paired,
    staged,
    lined,
    crossed,
    cross_out,
    final_out,
    final_in,
    local_sem,
    y_s,
    y_r,
    x_s,
    x_r,
    yx_s,
    yx_r,
    xy_s,
    xy_r,
    core_s,
    core_r,
    z_s,
    z_r,
    yl_s,
    yl_r,
    end_s,
    end_r,
):
    x, h, yl, z, c = place()
    half, width = grad_ref.shape
    tokens = 2 * half
    rows = half // NX
    split = 384
    g = x * 2 + h
    v = yl * 16 + z * 2 + c
    goal_g, goal_v = z, 4 * g + 2 * yl + c
    from_g, from_v = v // 4, ((v % 4) // 2) * 16 + g * 2 + v % 2
    moves = (goal_g != g) | (goal_v != v)
    partner = device(x, 1 - h, yl, z, c)
    mate = device(x, h, yl, z, 1 - c)
    across = device(x, h, 1 - yl, z, c)
    barrier = pltpu.get_barrier_semaphore()
    peers = [partner, mate, across]
    peers += [device((x + dx) % NX, h, yl, z, c) for dx in (1, 3, 2)]
    peers += [device(x, h, yl, (z + dz) % NZ, c) for dz in range(1, NZ)]
    for peer in peers:
        pl.semaphore_signal(barrier, inc=1, device_id=peer, device_id_type=MESH)

    @pl.when(moves)
    def _():
        pl.semaphore_signal(
            barrier, inc=1, device_id={"grp": from_g, "vocab": from_v}, device_id_type=MESH
        )

    pl.semaphore_wait(barrier, len(peers) + jnp.where(moves, 1, 0))

    def spot(xs, hs, low=0, size=width):
        return every.at[xs, pl.ds(pl.multiple_of(hs * half, half), half), pl.ds(low, size)]

    pending = [send(grad_ref, spot(x, h), y_s, y_r, partner)]
    for k, dx in enumerate((1, 3, 2)):
        pending.append(
            send(grad_ref, spot(x, h), x_s.at[k], x_r.at[k], device((x + dx) % NX, h, yl, z, c))
        )
    keep = pltpu.make_async_copy(grad_ref, spot(x, h), local_sem)
    keep.start()
    turned[...] = jnp.transpose(own_ref[...])
    rows_acc[...] = jnp.zeros_like(rows_acc)
    keep.wait()
    arrived(spot(x, 1 - h), y_r)
    for k, dx in enumerate((1, 3, 2)):
        tail = spot(x, 1 - h, split, width - split)
        pending.append(send(tail, tail, yx_s.at[k], yx_r.at[k], device((x + dx) % NX, h, yl, z, c)))

    def rows_part(xs):
        head = weight_ref[:, pl.ds(pl.multiple_of(xs * width, TILE), width)]

        def body(i, carry):
            span = pl.ds(pl.multiple_of(i * 256, 256), 256)
            out = lax.dot_general(
                every[xs, span, :], head, (((1,), (1,)), ((), ())), preferred_element_type=jnp.float32
            )
            for s in range(4):
                rows_acc[s, span, :] += out[:, s * TILE : (s + 1) * TILE]
            return carry

        lax.fori_loop(0, tokens // 256, body, 0)

    def head_part(xs):
        def body(i, carry):
            span = pl.ds(pl.multiple_of(i * 256, 256), 256)
            out = jnp.dot(turned[span, :], every[xs], preferred_element_type=jnp.float32)
            head_ref[span, pl.ds(pl.multiple_of(xs * width, TILE), width)] = out.astype(jnp.bfloat16)
            return carry

        lax.fori_loop(0, turned.shape[0] // 256, body, 0)

    rows_part(x)
    head_part(x)
    for k, dx in enumerate((1, 3, 2)):
        xs = (x - dx + NX) % NX
        arrived(spot(xs, h), x_r.at[k])
        lead = spot(xs, h, 0, split)
        pending.append(send(lead, lead, xy_s.at[k], xy_r.at[k], partner))
    for k, dx in enumerate((1, 3, 2)):
        xs = (x - dx + NX) % NX
        arrived(spot(xs, 1 - h, split, width - split), yx_r.at[k])
        arrived(spot(xs, 1 - h, 0, split), xy_r.at[k])
        rows_part(xs)
        if k < 2:
            head_part(xs)
    for b in range(NYL):
        pending.append(
            send(rows_acc.at[2 * b + 1 - c], paired.at[b], core_s.at[b], core_r.at[b], mate)
        )
    head_part((x - 2 + NX) % NX)
    for b in range(NYL):
        arrived(paired.at[b], core_r.at[b])

    def gather(t, carry):
        start = pl.multiple_of((t % 2) * half + (t // 2) * rows, rows)
        for b in range(NYL):
            staged[t, b] = rows_acc[2 * b + c, pl.ds(start, rows), :] + paired[b, pl.ds(start, rows), :]
        return carry

    lax.fori_loop(0, NZ, gather, 0)
    for dz in range(1, NZ):
        zt = (z + dz) % NZ
        pending.append(
            send(staged.at[zt], lined.at[dz], z_s.at[dz], z_r.at[dz], device(x, h, yl, zt, c))
        )
    for dz in range(1, NZ):
        arrived(lined.at[dz], z_r.at[dz])
    total = staged[z]
    for dz in range(1, NZ):
        total = total + lined[dz]
    lined[0] = total
    cross_out[...] = lined[0, 1 - yl]
    pending.append(send(cross_out, crossed, yl_s, yl_r, across))
    arrived(crossed, yl_r)
    final_out[...] = (lined[0, yl] + crossed[...]).astype(jnp.bfloat16)

    @pl.when(moves)
    def _():
        last = send(final_out, final_in, end_s, end_r, {"grp": goal_g, "vocab": goal_v})
        last.wait()
        hidden_ref[...] = final_in[...]

    @pl.when(jnp.logical_not(moves))
    def _():
        hidden_ref[...] = final_out[...]

    for copy in pending:
        copy.wait_send()


def dma(*shape):
    return pltpu.SemaphoreType.DMA(shape)


def shards(hidden, weight, teacher_panels, token_ids, row_counts):
    rows, model = hidden.shape
    depth, slab = weight.shape
    width = -(-slab // (NX * TILE)) * TILE
    extra = NX * width - slab
    half, tokens = NX * rows, NX * NH * rows
    padded = jnp.pad(weight, ((0, 0), (0, extra)))
    teacher = jnp.stack(
        [
            jnp.pad(teacher_panels[:, :slab], ((0, 0), (0, extra))),
            jnp.pad(teacher_panels[:, slab:], ((0, 0), (0, extra))),
        ]
    )
    meta = jnp.concatenate(
        [
            token_ids.astype(jnp.float32)[None],
            jnp.broadcast_to(row_counts.astype(jnp.float32)[:, None], (7, rows)),
        ]
    )
    chunks = []
    low = 0
    while low < width:
        chunks.append((low, min(256, width - low)))
        low += 256
    n, m, q = len(GROUP_PEERS), len(PAIR_PEERS), len(LINE_PEERS)
    vmem = pl.BlockSpec(memory_space=pltpu.VMEM)
    f32, bf16 = jnp.float32, jnp.bfloat16
    grad, own, kl = pl.pallas_call(
        functools.partial(loss_kernel, slab, tuple(chunks)),
        name="loss",
        out_shape=[
            jax.ShapeDtypeStruct((half, width), bf16),
            jax.ShapeDtypeStruct((tokens, depth), bf16),
            jax.ShapeDtypeStruct((1, rows), f32),
        ],
        in_specs=[vmem] * 4,
        out_specs=[vmem] * 3,
        scratch_shapes=[
            pltpu.VMEM((tokens, NX * depth), bf16),
            pltpu.VMEM((NX * depth, width), bf16),
            pltpu.VMEM((half, width), f32),
            pltpu.VMEM((half, width), f32),
            pltpu.VMEM((half, width), f32),
            pltpu.VMEM((half, width), bf16),
            pltpu.VMEM((NX * NH, 8, rows), f32),
            pltpu.VMEM((m + 1, NX, 8, rows), f32),
            pltpu.VMEM((q + 1, NX, 8, rows), f32),
            pltpu.VMEM((NX, 8, rows), f32),
            pltpu.VMEM((half, TILE), f32),
            dma(NX + 2),
            dma(n), dma(n), dma(n), dma(n), dma(2 * n), dma(2 * n), dma(n), dma(n),
            dma(3 * len(chunks)), dma(3 * len(chunks)), dma(len(chunks)), dma(len(chunks)),
            dma(m), dma(m), dma(m), dma(m), dma(q), dma(q),
        ],
        compiler_params=pltpu.CompilerParams(
            collective_id=1, has_side_effects=True, vmem_limit_bytes=56 * 2**20
        ),
    )(hidden, padded, teacher, meta)
    head_grad, hidden_grad = pl.pallas_call(
        grads_kernel,
        name="grads",
        out_shape=[
            jax.ShapeDtypeStruct((depth, NX * width), bf16),
            jax.ShapeDtypeStruct((rows, TILE), bf16),
        ],
        in_specs=[vmem] * 3,
        out_specs=[vmem] * 2,
        scratch_shapes=[
            pltpu.VMEM((NX, tokens, width), bf16),
            pltpu.VMEM((depth, tokens), bf16),
            pltpu.VMEM((4, tokens, TILE), f32),
            pltpu.VMEM((NYL, tokens, TILE), f32),
            pltpu.VMEM((NZ, NYL, rows, TILE), f32),
            pltpu.VMEM((NZ, NYL, rows, TILE), f32),
            pltpu.VMEM((rows, TILE), f32),
            pltpu.VMEM((rows, TILE), f32),
            pltpu.VMEM((rows, TILE), bf16),
            pltpu.VMEM((rows, TILE), bf16),
            pltpu.SemaphoreType.DMA,
            pltpu.SemaphoreType.DMA, pltpu.SemaphoreType.DMA,
            dma(3), dma(3), dma(3), dma(3), dma(3), dma(3),
            dma(NYL), dma(NYL), dma(NZ), dma(NZ),
            pltpu.SemaphoreType.DMA, pltpu.SemaphoreType.DMA,
            pltpu.SemaphoreType.DMA, pltpu.SemaphoreType.DMA,
        ],
        compiler_params=pltpu.CompilerParams(
            collective_id=2, has_side_effects=True, vmem_limit_bytes=56 * 2**20
        ),
    )(grad, own, padded)
    return kl[0], hidden_grad, head_grad[:, :slab]


def solution(mesh):
    return jax.shard_map(
        shards,
        mesh=mesh,
        in_specs=(P("grp", None), P("grp", "vocab"), P("grp", "vocab"), P("grp"), P("grp")),
        out_specs=(P("grp"), P("grp", "vocab"), P("grp", "vocab")),
        check_vma=False,
    )
```

```python
import functools

import jax
import jax.numpy as jnp
from jax import lax
from jax.experimental import pallas as pl
from jax.experimental.pallas import tpu as pltpu
from jax.sharding import PartitionSpec as P

KL_SCALE = 256.0
MESH = pl.DeviceIdType.MESH
LOW = -1e30
NX, NH, NYL, NZ, NC = 4, 2, 2, 8, 2
TILE = 128
GROUP_PEERS = [(dx, dh) for dh in (1, 0) for dx in (1, 3, 2, 0) if dx or dh]
PAIR_PEERS = [(dx, dc) for dc in (0, 1) for dx in (1, 3, 2, 0) if dx or dc]
LINE_PEERS = [(dy, dz) for dy in (0, 1) for dz in range(NZ) if dy or dz]


def place():
    g = lax.axis_index("grp")
    v = lax.axis_index("vocab")
    return g // 2, g % 2, v // 16, (v // 2) % 8, v % 2


def device(x, h, yl, z, c):
    return {"grp": x * 2 + h, "vocab": yl * 16 + z * 2 + c}


def to_columns(tile):
    return jnp.transpose(jnp.concatenate([tile] * (TILE // 8), axis=0))


def merge(buf):
    peak_s = jnp.max(buf[:, :, 0], axis=0)
    scale_s = jnp.exp(buf[:, :, 0] - peak_s[None])
    peak_t = jnp.max(buf[:, :, 3], axis=0)
    scale_t = jnp.exp(buf[:, :, 3] - peak_t[None])
    return [
        peak_s,
        jnp.sum(buf[:, :, 1] * scale_s, axis=0),
        jnp.sum(buf[:, :, 2] * scale_s, axis=0),
        peak_t,
        jnp.sum(buf[:, :, 4] * scale_t, axis=0),
        jnp.sum(buf[:, :, 5], axis=0),
        jnp.sum(buf[:, :, 6], axis=0),
    ]


def fused_kernel(
    slab,
    chunks,
    hidden_ref,
    weight_ref,
    panel_ref,
    token_ref,
    count_ref,
    head_ref,
    out_ref,
    kl_ref,
    padded,
    wide,
    heads,
    partial,
    landed,
    logits,
    teacher,
    teach,
    meta,
    metas,
    near,
    far,
    outcome,
    cols,
    every,
    rows_out,
    paired,
    staged,
    lined,
    cross_out,
    crossed,
    final_out,
    final_in,
    local_sem,
    sent,
    got,
    z_sent,
    z_got,
    end_sem,
):
    x, h, yl, z, c = place()
    rows, depth = hidden_ref.shape[0], padded.shape[1]
    above = GROUP_PEERS[:NX]
    beside = GROUP_PEERS[NX:]
    half = NX * rows
    width = padded.shape[0] // NX
    z_pair = z + 1 - 2 * lax.rem(z, 2)
    g = x * 2 + h
    v = yl * 16 + z * 2 + c
    goal_g, goal_v = z, 4 * g + 2 * yl + c
    from_g, from_v = v // 4, ((v % 4) // 2) * 16 + g * 2 + v % 2
    moves = (goal_g != g) | (goal_v != v)
    partner = device(x, 1 - h, yl, z, c)
    mate = device(x, h, yl, z, 1 - c)
    across = device(x, h, 1 - yl, z, c)
    right, left = (x + 1) % NX, (x + NX - 1) % NX
    opposite = (x + 2) % NX
    to_right, to_left = device(right, h, yl, z, c), device(left, h, yl, z, c)

    barrier = pltpu.get_barrier_semaphore()
    peers = [device((x + dx) % NX, (h + dh) % NH, yl, z, c) for dx, dh in GROUP_PEERS]
    peers += [device((x + dx) % NX, h, yl, z, 1 - c) for dx in range(NX)]
    peers += [device(x, h, (yl + dy) % NYL, (z + dz) % NZ, c) for dy, dz in LINE_PEERS]
    for peer in peers:
        pl.semaphore_signal(barrier, inc=1, device_id=peer, device_id_type=MESH)

    @pl.when(moves)
    def _():
        pl.semaphore_signal(
            barrier, inc=1, device_id={"grp": from_g, "vocab": from_v}, device_id_type=MESH
        )

    meta[...] = jnp.where(
        lax.broadcasted_iota(jnp.int32, meta.shape, 0) == 0,
        token_ref[...].astype(jnp.float32),
        count_ref[0].astype(jnp.float32),
    )
    metas[g] = meta[...]
    padded[0:slab, :] = weight_ref[...]
    padded[slab:, :] = jnp.zeros((NX * width - slab, depth), padded.dtype)
    pl.semaphore_wait(barrier, len(peers) + jnp.where(moves, 1, 0))

    pending = []

    def send(src, dst, target):
        slot = len(pending)
        copy = pltpu.make_async_remote_copy(
            src_ref=src, dst_ref=dst, send_sem=sent.at[slot], recv_sem=got.at[slot],
            device_id=target, device_id_type=MESH,
        )
        copy.start()
        pending.append(copy)
        return slot

    def arrived(ref, slot):
        pltpu.make_async_copy(ref, ref, got.at[slot]).wait()

    parity = lax.rem(z, 2)
    mine, other = 2 * c + parity, 2 * c + 1 - parity

    def region(xs, hs, kx):
        return wide.at[
            pl.ds(pl.multiple_of(hs * half + xs * rows, rows), rows),
            pl.ds(pl.multiple_of(kx * depth, depth), depth),
        ]

    def block(kx, hs):
        return hidden_ref.at[:, pl.ds(pl.multiple_of((kx * 2 + hs) * depth, depth), depth)]

    hid = {}

    def spread(peers):
        for dx, dh in peers:
            xt, ht = (x + dx) % NX, (h + dh) % NH
            hid[dx, dh] = send(block(mine, ht), region(x, h, mine), device(xt, ht, yl, z, c))

    def weight_rows(xs, low, size):
        return pl.ds(pl.multiple_of(xs * width + low, TILE), size)

    def head_spot(kx, low, size):
        return heads.at[pl.ds(low, size), pl.ds(pl.multiple_of(kx * depth, depth), depth)]

    wgt = []

    def spread_weight():
        if len(wgt) < len(chunks):
            low, size = chunks[len(wgt)]
            wgt.append(
                [
                    send(
                        padded.at[weight_rows((x + dx) % NX, low, size), :],
                        head_spot(x, low, size),
                        device((x + dx) % NX, h, yl, z, c),
                    )
                    for dx in (1, 3, 2)
                ]
            )

    fwd, near_core, far_core, met = {}, {}, {}, {}

    def source(peer):
        return (x - peer[0] + NX) % NX, (h + peer[1]) % NH

    def pass_on(peers):
        for peer in peers:
            spot = region(*source(peer), mine)
            arrived(spot, hid[peer])
            fwd[peer] = send(spot, spot, device(x, h, yl, z_pair, c))
            near_core[peer] = send(spot, spot, mate)

    def pass_core(peers):
        for peer in peers:
            spot = region(*source(peer), other)
            arrived(spot, fwd[peer])
            far_core[peer] = send(spot, spot, mate)

    def collect(peers):
        for peer in peers:
            xs, hs = source(peer)
            arrived(region(xs, hs, 2 * (1 - c) + parity), near_core[peer])
            arrived(region(xs, hs, 2 * (1 - c) + 1 - parity), far_core[peer])

    spread(above)
    spread_weight()
    for dx, dh in GROUP_PEERS:
        met[dx, dh] = send(meta, metas.at[g], device((x + dx) % NX, (h + dh) % NH, yl, z, c))
    locals_ = [
        pltpu.make_async_copy(block(kx, h), region(x, h, kx), local_sem.at[kx]) for kx in range(NX)
    ]
    locals_.append(
        pltpu.make_async_copy(
            padded.at[weight_rows(x, 0, width), :], head_spot(x, 0, width), local_sem.at[NX]
        )
    )
    for copy in locals_:
        copy.start()

    teacher[...] = jnp.zeros_like(teacher)
    for side in range(NC):
        teacher[side, :, 0:slab] = panel_ref[:, side * slab : (side + 1) * slab]

    pass_on(above)
    spread_weight()
    pass_core(above)
    spread_weight()
    spread(beside)
    for copy in locals_:
        copy.wait()
    for peer in GROUP_PEERS:
        xs, hs = source(peer)
        arrived(metas.at[xs * 2 + hs], met[peer])
    collect(above)

    def product(side, low, size):
        return lax.dot_general(
            wide[pl.ds(pl.multiple_of(side * half, half), half), :],
            heads[low : low + size, :],
            (((1,), (1,)), ((), ())),
            preferred_element_type=jnp.float32,
        )

    def teach_spot(xs, cs):
        step = rows // 2
        return teach.at[pl.ds(pl.multiple_of(xs * rows + cs * step, step), step), :]

    def teacher_piece(xt, ct):
        return teacher.at[ct, :, pl.ds(pl.multiple_of(xt * width, TILE), width)]

    halves, teaching = [], []
    for j, (low, size) in enumerate(chunks):
        for k, dx in enumerate((1, 3, 2)):
            arrived(head_spot((x - dx + NX) % NX, low, size), wgt[j][k])
        partial[:, low : low + size] = product(1 - h, low, size)
        piece = pl.ds(low, size)
        halves.append(send(partial.at[:, piece], landed.at[:, piece], partner))
        spread_weight()
        if j == 1:
            pass_on(beside)
        if j == 2:
            pass_core(beside)
        if j == len(chunks) - 2:
            keep = pltpu.make_async_copy(teacher_piece(x, c), teach_spot(x, c), local_sem.at[0])
            keep.start()
            for dx, dc in PAIR_PEERS:
                xt, ct = (x + dx) % NX, (c + dc) % NC
                teaching.append(send(teacher_piece(xt, ct), teach_spot(x, c), device(xt, h, yl, z, ct)))
    collect(beside)
    for low in range(0, width, 256):
        size = min(256, width - low)
        logits[:, low : low + size] = product(h, low, size)

    step = rows // 2
    lane = lax.broadcasted_iota(jnp.int32, (step, TILE), 1)
    column = lax.broadcasted_iota(jnp.int32, (step, width), 1)
    inside = column < slab - x * width
    base = (v * slab + x * width).astype(jnp.float32)
    column_f = column.astype(jnp.float32)

    def fill(group, carry):
        cols[pl.ds(pl.multiple_of(group * rows, rows), rows), :] = to_columns(metas[group * 2 + h])
        return carry

    lax.fori_loop(0, NX, fill, 0)
    keep.wait()
    for k, (dx, dc) in enumerate(PAIR_PEERS):
        arrived(teach_spot((x - dx + NX) % NX, (c + dc) % NC), teaching[k])

    def measure_teacher(i, carry):
        span = pl.ds(pl.multiple_of(i * step, step), step)
        raw = teach[span, :].astype(jnp.float32)
        masked = jnp.where(inside, raw, LOW)
        old = cols[span, :]
        chosen = (column_f == old[:, 0:1] - base) & inside
        peak = jnp.max(masked, axis=1, keepdims=True)
        total = jnp.sum(jnp.exp(masked - peak), axis=1, keepdims=True)
        pick = jnp.sum(jnp.where(chosen, raw, 0.0), axis=1, keepdims=True)
        table = jnp.where(lane == 4, peak, jnp.where(lane == 5, total, pick))
        cols[span, :] = jnp.where(lane == 0, old, table)
        return carry

    lax.fori_loop(0, half // step, measure_teacher, 0)
    for j, (low, size) in enumerate(chunks):
        arrived(landed.at[:, pl.ds(low, size)], halves[j])

    def measure_student(i, carry):
        span = pl.ds(pl.multiple_of(i * step, step), step)
        student = jnp.where(inside, logits[span, :] + landed[span, :], LOW)
        logits[span, :] = student
        raw = teach[span, :].astype(jnp.float32)
        old = cols[span, :]
        chosen = (column_f == old[:, 0:1] - base) & inside
        peak = jnp.max(student, axis=1, keepdims=True)
        exps = jnp.exp(student - peak)
        found = {
            1: peak,
            2: jnp.sum(exps, axis=1, keepdims=True),
            3: jnp.sum(exps * (student - raw), axis=1, keepdims=True),
            6: jnp.sum(jnp.where(chosen, student, 0.0), axis=1, keepdims=True),
        }
        for k, value in found.items():
            old = jnp.where(lane == k, value, old)
        cols[span, :] = old
        return carry

    lax.fori_loop(0, half // step, measure_student, 0)

    def pack(group, carry):
        table = jnp.transpose(cols[pl.ds(pl.multiple_of(group * rows, rows), rows), :])
        near[0, group] = table[0:8]
        return carry

    lax.fori_loop(0, NX, pack, 0)
    slots = [
        send(near.at[0], near.at[k + 1], device((x + dx) % NX, h, yl, z, (c + dc) % NC))
        for k, (dx, dc) in enumerate(PAIR_PEERS)
    ]
    for k, slot in enumerate(slots):
        arrived(near.at[k + 1], slot)
    for k, value in enumerate(merge(near[:, :, 1:8])):
        far[0, :, k] = value
    token_row = near[0, :, 0]
    far[0, :, 7] = token_row
    slots = [
        send(far.at[0], far.at[k + 1], device(x, h, (yl + dy) % NYL, (z + dz) % NZ, c))
        for k, (dy, dz) in enumerate(LINE_PEERS)
    ]
    for k, slot in enumerate(slots):
        arrived(far.at[k + 1], slot)
    peak_s, sum_s, weighted, peak_t, sum_t, pick_s, pick_t = merge(far[...])

    total_rows = jnp.sum(metas[:, 1, 0:1])
    student_norm = peak_s + jnp.log(sum_s)
    teacher_norm = peak_t + jnp.log(sum_t)
    mean_gap = weighted / sum_s
    divergence = mean_gap - student_norm + teacher_norm
    advantage = (pick_t - teacher_norm) - (pick_s - student_norm)
    counts = jnp.stack([metas[group * 2 + h][1] for group in range(NX)], axis=0)
    valid = lax.broadcasted_iota(jnp.int32, (NX, rows), 1).astype(jnp.float32) < counts
    row_weight = jnp.where(valid, rows / total_rows, 0.0)
    kl = jnp.where(valid, divergence, 0.0)
    own_group = lax.broadcasted_iota(jnp.int32, (NX, rows), 0) == x
    kl_ref[...] = jnp.sum(jnp.where(own_group, kl, 0.0), axis=0, keepdims=True)
    table = [
        peak_s, 1.0 / sum_s, mean_gap, row_weight * KL_SCALE, row_weight * advantage, token_row,
        token_row, token_row,
    ]
    for k, value in enumerate(table):
        outcome[:, k] = value

    def place_of(xs, hs, p, low=0, size=None):
        start = pl.multiple_of(hs * half + p * rows + low, step)
        return every.at[xs, pl.ds(start, rows if size is None else size), :]

    own_start = h * half

    def finish(i, carry):
        span = pl.ds(pl.multiple_of(i * step, step), step)
        student = logits[span, :]
        raw = teach[span, :].astype(jnp.float32)
        table = cols[span, :]
        probs = jnp.exp(student - table[:, 0:1]) * table[:, 1:2]
        chosen = (column_f == table[:, 5:6] - base) & inside
        adv = table[:, 4:5]
        grad = probs * (table[:, 3:4] * ((student - raw) - table[:, 2:3]) + adv)
        grad = grad - jnp.where(chosen, adv, 0.0)
        every[x, pl.ds(pl.multiple_of(own_start + i * step, step), step), :] = grad.astype(jnp.bfloat16)
        return carry

    direct = []

    def spread_grad():
        if len(direct) < NX:
            spot = place_of(x, h, len(direct))
            direct.append([send(spot, spot, to_right), send(spot, spot, to_left), send(spot, spot, partner)])

    per = rows // step
    for p in range(NX):
        cols[p * rows : (p + 1) * rows, :] = to_columns(outcome[p])
        lax.fori_loop(p * per, (p + 1) * per, finish, 0)
        if p < 2:
            spread_grad()

    def rows_part(p):
        for side in range(NH):
            start = side * half + p * rows
            out = jnp.zeros((rows, depth), jnp.float32)
            for xs in range(NX):
                out = out + jnp.dot(
                    every[xs, start : start + rows, :],
                    padded[xs * width : (xs + 1) * width, :],
                    preferred_element_type=jnp.float32,
                )
            for s in range(4):
                rows_out[p, s % 2, s // 2, side] = out[:, s * TILE : (s + 1) * TILE]
        return send(rows_out.at[p, 1 - c], paired.at[p], mate)

    def line_up(p, slot):
        arrived(paired.at[p], slot)
        for side in range(NH):
            t = 2 * p + side
            for b in range(NYL):
                staged[t, b] = rows_out[p, c, b, side] + paired[p, b, side]

            @pl.when(z != t)
            def _():
                pltpu.make_async_remote_copy(
                    src_ref=staged.at[t], dst_ref=lined.at[z], send_sem=z_sent.at[t],
                    recv_sem=z_got.at[z], device_id=device(x, h, yl, t, c), device_id_type=MESH,
                ).start()

    far_own, last, paired_slots = [], [], []
    for p in range(NX + 3):
        if p < NX:
            arrived(place_of(left, h, p), direct[p][0])
            lead = place_of(left, h, p, 0, step)
            a = send(lead, lead, to_right)
            arrived(place_of(right, h, p), direct[p][1])
            tail = place_of(right, h, p, step, step)
            far_own.append((a, send(tail, tail, to_left)))
            spot = place_of(x, 1 - h, p)
            arrived(spot, direct[p][2])
            last.append([send(spot, spot, to_right), send(spot, spot, to_left)])
            spread_grad()
        if 1 <= p <= NX:
            q = p - 1
            arrived(place_of(opposite, h, q, 0, step), far_own[q][0])
            arrived(place_of(opposite, h, q, step, step), far_own[q][1])
            spot = place_of(opposite, h, q)
            last[q].append(send(spot, spot, partner))
        if 2 <= p <= NX + 1:
            q = p - 2
            arrived(place_of(left, 1 - h, q), last[q][0])
            arrived(place_of(right, 1 - h, q), last[q][1])
            arrived(place_of(opposite, 1 - h, q), last[q][2])
            paired_slots.append(rows_part(q))
        if 3 <= p:
            line_up(p - 3, paired_slots[p - 3])

    for xs in range(NX):
        size = min(width, slab - xs * width)
        out = lax.dot_general(
            every[xs],
            wide[:, pl.ds(pl.multiple_of(x * depth, depth), depth)],
            (((0,), (0,)), ((), ())),
            preferred_element_type=jnp.float32,
        )
        head_ref[xs * width : xs * width + size, :] = out[:size].astype(jnp.bfloat16)
    lined[z] = staged[z]
    for s in range(NZ):

        @pl.when(z != s)
        def _():
            pltpu.make_async_copy(lined.at[s], lined.at[s], z_got.at[s]).wait()

    total = lined[0]
    for s in range(1, NZ):
        total = total + lined[s]
    staged[z] = total
    cross_out[...] = staged[z, 1 - yl]
    slot = send(cross_out, crossed, across)
    arrived(crossed, slot)
    final_out[...] = (staged[z, yl] + crossed[...]).astype(jnp.bfloat16)

    @pl.when(moves)
    def _():
        copy = pltpu.make_async_remote_copy(
            src_ref=final_out, dst_ref=final_in, send_sem=end_sem.at[0], recv_sem=end_sem.at[1],
            device_id={"grp": goal_g, "vocab": goal_v}, device_id_type=MESH,
        )
        copy.start()
        copy.wait()
        out_ref[...] = final_in[...]

    @pl.when(jnp.logical_not(moves))
    def _():
        out_ref[...] = final_out[...]

    for copy in pending:
        copy.wait_send()
    for t in range(NZ):

        @pl.when(z != t)
        def _():
            pltpu.make_async_copy(staged.at[t], staged.at[t], z_sent.at[t]).wait()


def shards(hidden, weight, teacher_panels, token_ids, row_counts):
    rows = hidden.shape[0]
    depth, slab = weight.shape
    width = -(-slab // (NX * TILE)) * TILE
    half, tokens = NX * rows, NX * NH * rows
    chunks = tuple((low, TILE) for low in range(0, width, TILE))
    m, q = len(PAIR_PEERS), len(LINE_PEERS)
    vmem = pl.BlockSpec(memory_space=pltpu.VMEM)
    f32, bf16 = jnp.float32, jnp.bfloat16
    copies = 5 * len(GROUP_PEERS) + 4 * len(chunks) + 2 * m + q + 9 * NX + 1
    head_grad, hidden_grad, kl = pl.pallas_call(
        functools.partial(fused_kernel, slab, chunks),
        name="distill",
        out_shape=[
            jax.ShapeDtypeStruct((slab, depth), bf16),
            jax.ShapeDtypeStruct((rows, TILE), bf16),
            jax.ShapeDtypeStruct((1, rows), f32),
        ],
        in_specs=[vmem] * 4 + [pl.BlockSpec(memory_space=pltpu.SMEM)],
        out_specs=[vmem] * 3,
        scratch_shapes=[
            pltpu.VMEM((NX * width, depth), bf16),
            pltpu.VMEM((tokens, NX * depth), bf16),
            pltpu.VMEM((width, NX * depth), bf16),
            pltpu.VMEM((half, width), f32),
            pltpu.VMEM((half, width), f32),
            pltpu.VMEM((half, width), f32),
            pltpu.VMEM((NC, rows // 2, NX * width), bf16),
            pltpu.VMEM((half, width), bf16),
            pltpu.VMEM((8, rows), f32),
            pltpu.VMEM((NX * NH, 8, rows), f32),
            pltpu.VMEM((m + 1, NX, 8, rows), f32),
            pltpu.VMEM((q + 1, NX, 8, rows), f32),
            pltpu.VMEM((NX, 8, rows), f32),
            pltpu.VMEM((half, TILE), f32),
            pltpu.VMEM((NX, tokens, width), bf16),
            pltpu.VMEM((NX, NC, NYL, NH, rows, TILE), f32),
            pltpu.VMEM((NX, NYL, NH, rows, TILE), f32),
            pltpu.VMEM((NZ, NYL, rows, TILE), f32),
            pltpu.VMEM((NZ, NYL, rows, TILE), f32),
            pltpu.VMEM((rows, TILE), f32),
            pltpu.VMEM((rows, TILE), f32),
            pltpu.VMEM((rows, TILE), bf16),
            pltpu.VMEM((rows, TILE), bf16),
            pltpu.SemaphoreType.DMA((NX + 1,)),
            pltpu.SemaphoreType.DMA((copies,)),
            pltpu.SemaphoreType.DMA((copies,)),
            pltpu.SemaphoreType.DMA((NZ,)),
            pltpu.SemaphoreType.DMA((NZ,)),
            pltpu.SemaphoreType.DMA((2,)),
        ],
        compiler_params=pltpu.CompilerParams(
            collective_id=1, has_side_effects=True, vmem_limit_bytes=56 * 2**20
        ),
    )(hidden, weight.T, teacher_panels, token_ids[None], row_counts)
    return kl[0], hidden_grad, head_grad.T


def solution(mesh):
    return jax.shard_map(
        shards,
        mesh=mesh,
        in_specs=(P("grp", None), P("grp", "vocab"), P("grp", "vocab"), P("grp"), P("grp")),
        out_specs=(P("grp"), P("grp", "vocab"), P("grp", "vocab")),
        check_vma=False,
    )
```

```python
import functools

import jax
import jax.numpy as jnp
from jax import lax
from jax.experimental import pallas as pl
from jax.experimental.pallas import tpu as pltpu
from jax.sharding import PartitionSpec as P

KL_SCALE = 256.0
MESH = pl.DeviceIdType.MESH
LOW = -1e30
NX, NH, NYL, NZ, NC = 4, 2, 2, 8, 2
TILE = 128
GROUP_PEERS = [(dx, dh) for dh in (1, 0) for dx in (0, 1, 3, 2) if dx or dh]
PAIR_PEERS = [(dx, dc) for dc in (0, 1) for dx in (1, 3, 2, 0) if dx or dc]
LINE_PEERS = [(dy, dz) for dy in (0, 1) for dz in range(NZ) if dy or dz]


def place():
    g = lax.axis_index("grp")
    v = lax.axis_index("vocab")
    return g // 2, g % 2, v // 16, (v // 2) % 8, v % 2


def device(x, h, yl, z, c):
    return {"grp": x * 2 + h, "vocab": yl * 16 + z * 2 + c}


def to_columns(tile):
    return jnp.transpose(jnp.concatenate([tile] * (TILE // 8), axis=0))


def merge(buf):
    peak_s = jnp.max(buf[:, :, 0], axis=0)
    scale_s = jnp.exp(buf[:, :, 0] - peak_s[None])
    peak_t = jnp.max(buf[:, :, 3], axis=0)
    scale_t = jnp.exp(buf[:, :, 3] - peak_t[None])
    return [
        peak_s,
        jnp.sum(buf[:, :, 1] * scale_s, axis=0),
        jnp.sum(buf[:, :, 2] * scale_s, axis=0),
        peak_t,
        jnp.sum(buf[:, :, 4] * scale_t, axis=0),
        jnp.sum(buf[:, :, 5], axis=0),
        jnp.sum(buf[:, :, 6], axis=0),
    ]


def fused_kernel(
    slab,
    chunks,
    hidden_ref,
    weight_ref,
    panel_ref,
    token_ref,
    count_ref,
    head_ref,
    out_ref,
    kl_ref,
    padded,
    wide,
    heads,
    partial,
    landed,
    logits,
    teacher,
    teach,
    meta,
    metas,
    near,
    far,
    outcome,
    cols,
    every,
    own,
    rows_out,
    paired,
    staged,
    lined,
    cross_out,
    final_in,
    local_sem,
    sent,
    got,
    end_sent,
    end_got,
):
    x, h, yl, z, c = place()
    rows, depth = hidden_ref.shape[0], padded.shape[1]
    above = GROUP_PEERS[:NX]
    beside = GROUP_PEERS[NX:]
    half = NX * rows
    width = padded.shape[0] // NX
    z_pair = z + 1 - 2 * lax.rem(z, 2)
    g = x * 2 + h
    v = yl * 16 + z * 2 + c
    part = rows * NH // NZ
    quarter = lax.rem(z, 4)
    goals = {(p, b): (2 * p + z // 4, 4 * g + 2 * b + c) for p in range(NX) for b in range(NYL)}
    origins = {
        (b, k): (v // 4, b * 16 + ((g % 2) * 4 + k) * 2 + v % 2) for b in range(NYL) for k in range(4)
    }
    leaves = {key: (a != g) | (b != v) for key, (a, b) in goals.items()}
    comes = {key: (a != g) | (b != v) for key, (a, b) in origins.items()}
    partner = device(x, 1 - h, yl, z, c)
    mate = device(x, h, yl, z, 1 - c)
    right, left = (x + 1) % NX, (x + NX - 1) % NX
    opposite = (x + 2) % NX
    to_right, to_left = device(right, h, yl, z, c), device(left, h, yl, z, c)

    barrier = pltpu.get_barrier_semaphore()
    peers = [device((x + dx) % NX, (h + dh) % NH, yl, z, c) for dx, dh in GROUP_PEERS]
    peers += [device((x + dx) % NX, h, yl, z, 1 - c) for dx in range(NX)]
    peers += [device(x, h, (yl + dy) % NYL, (z + dz) % NZ, c) for dy, dz in LINE_PEERS]
    for peer in peers:
        pl.semaphore_signal(barrier, inc=1, device_id=peer, device_id_type=MESH)

    for key, (a, b) in origins.items():

        @pl.when(comes[key])
        def _():
            pl.semaphore_signal(
                barrier, inc=1, device_id={"grp": a, "vocab": b}, device_id_type=MESH
            )

    meta[...] = jnp.where(
        lax.broadcasted_iota(jnp.int32, meta.shape, 0) == 0,
        token_ref[...].astype(jnp.float32),
        count_ref[0].astype(jnp.float32),
    )
    metas[g] = meta[...]
    padded[0:slab, :] = weight_ref[...]
    padded[slab:, :] = jnp.zeros((NX * width - slab, depth), padded.dtype)
    others = sum(jnp.where(leave, 1, 0) for leave in leaves.values())
    pl.semaphore_wait(barrier, len(peers) + others)

    pending = []

    def send(src, dst, target):
        slot = len(pending)
        copy = pltpu.make_async_remote_copy(
            src_ref=src, dst_ref=dst, send_sem=sent.at[slot], recv_sem=got.at[slot],
            device_id=target, device_id_type=MESH,
        )
        copy.start()
        pending.append(copy)
        return slot

    def arrived(ref, slot):
        pltpu.make_async_copy(ref, ref, got.at[slot]).wait()

    parity = lax.rem(z, 2)
    mine, other = 2 * c + parity, 2 * c + 1 - parity

    def region(xs, hs, kx):
        return wide.at[
            pl.ds(pl.multiple_of(hs * half + xs * rows, rows), rows),
            pl.ds(pl.multiple_of(kx * depth, depth), depth),
        ]

    def block(kx, hs):
        return hidden_ref.at[:, pl.ds(pl.multiple_of((kx * 2 + hs) * depth, depth), depth)]

    hid = {}

    def spread(peers):
        for dx, dh in peers:
            xt, ht = (x + dx) % NX, (h + dh) % NH
            hid[dx, dh] = send(block(mine, ht), region(x, h, mine), device(xt, ht, yl, z, c))

    def weight_rows(xs, low, size):
        return pl.ds(pl.multiple_of(xs * width + low, TILE), size)

    def head_spot(kx, low, size):
        return heads.at[pl.ds(low, size), pl.ds(pl.multiple_of(kx * depth, depth), depth)]

    wgt = []

    def spread_weight():
        if len(wgt) < len(chunks):
            low, size = chunks[len(wgt)]
            wgt.append(
                [
                    send(
                        padded.at[weight_rows((x + dx) % NX, low, size), :],
                        head_spot(x, low, size),
                        device((x + dx) % NX, h, yl, z, c),
                    )
                    for dx in (1, 3, 2)
                ]
            )

    fwd, near_core, far_core, met = {}, {}, {}, {}

    def source(peer):
        return (x - peer[0] + NX) % NX, (h + peer[1]) % NH

    def pass_on(peers):
        for peer in peers:
            spot = region(*source(peer), mine)
            arrived(spot, hid[peer])
            fwd[peer] = send(spot, spot, device(x, h, yl, z_pair, c))
            near_core[peer] = send(spot, spot, mate)

    def pass_core(peers):
        for peer in peers:
            spot = region(*source(peer), other)
            arrived(spot, fwd[peer])
            far_core[peer] = send(spot, spot, mate)

    def collect(peers):
        for peer in peers:
            xs, hs = source(peer)
            arrived(region(xs, hs, 2 * (1 - c) + parity), near_core[peer])
            arrived(region(xs, hs, 2 * (1 - c) + 1 - parity), far_core[peer])

    spread(above)
    spread_weight()
    spread_weight()
    for dx, dh in GROUP_PEERS:
        met[dx, dh] = send(meta, metas.at[g], device((x + dx) % NX, (h + dh) % NH, yl, z, c))
    locals_ = [
        pltpu.make_async_copy(block(kx, h), region(x, h, kx), local_sem.at[kx]) for kx in range(NX)
    ]
    locals_.append(
        pltpu.make_async_copy(
            padded.at[weight_rows(x, 0, width), :], head_spot(x, 0, width), local_sem.at[NX]
        )
    )
    for copy in locals_:
        copy.start()

    teacher[...] = jnp.zeros_like(teacher)
    for side in range(NC):
        teacher[side, :, 0:slab] = panel_ref[:, side * slab : (side + 1) * slab]

    pass_on(above)
    spread_weight()
    pass_core(above)
    spread(beside)
    spread_weight()
    for copy in locals_:
        copy.wait()
    for peer in GROUP_PEERS:
        xs, hs = source(peer)
        arrived(metas.at[xs * 2 + hs], met[peer])
    collect(above)

    def product(side, low, size):
        return lax.dot_general(
            wide[pl.ds(pl.multiple_of(side * half, half), half), :],
            heads[low : low + size, :],
            (((1,), (1,)), ((), ())),
            preferred_element_type=jnp.float32,
        )

    def teach_spot(xs, cs):
        step = rows // 2
        return teach.at[pl.ds(pl.multiple_of(xs * rows + cs * step, step), step), :]

    def teacher_piece(xt, ct):
        return teacher.at[ct, :, pl.ds(pl.multiple_of(xt * width, TILE), width)]

    halves, teaching = [], []
    for j, (low, size) in enumerate(chunks):
        for k, dx in enumerate((1, 3, 2)):
            arrived(head_spot((x - dx + NX) % NX, low, size), wgt[j][k])
        partial[:, low : low + size] = product(1 - h, low, size)
        piece = pl.ds(low, size)
        halves.append(send(partial.at[:, piece], landed.at[:, piece], partner))
        spread_weight()
        if j == 1:
            pass_on(beside)
        if j == 2:
            pass_core(beside)
        if j == len(chunks) - 2:
            keep = pltpu.make_async_copy(teacher_piece(x, c), teach_spot(x, c), local_sem.at[0])
            keep.start()
            for dx, dc in PAIR_PEERS:
                xt, ct = (x + dx) % NX, (c + dc) % NC
                teaching.append(send(teacher_piece(xt, ct), teach_spot(x, c), device(xt, h, yl, z, ct)))
    collect(beside)
    for low in range(0, width, 256):
        size = min(256, width - low)
        logits[:, low : low + size] = product(h, low, size)

    step = rows // 2
    lane = lax.broadcasted_iota(jnp.int32, (step, TILE), 1)
    column = lax.broadcasted_iota(jnp.int32, (step, width), 1)
    inside = column < slab - x * width
    base = (v * slab + x * width).astype(jnp.float32)
    column_f = column.astype(jnp.float32)

    def fill(group, carry):
        cols[pl.ds(pl.multiple_of(group * rows, rows), rows), :] = to_columns(metas[group * 2 + h])
        return carry

    lax.fori_loop(0, NX, fill, 0)
    keep.wait()
    for k, (dx, dc) in enumerate(PAIR_PEERS):
        arrived(teach_spot((x - dx + NX) % NX, (c + dc) % NC), teaching[k])

    def measure_teacher(i, carry):
        span = pl.ds(pl.multiple_of(i * step, step), step)
        raw = teach[span, :].astype(jnp.float32)
        masked = jnp.where(inside, raw, LOW)
        old = cols[span, :]
        chosen = (column_f == old[:, 0:1] - base) & inside
        peak = jnp.max(masked, axis=1, keepdims=True)
        total = jnp.sum(jnp.exp(masked - peak), axis=1, keepdims=True)
        pick = jnp.sum(jnp.where(chosen, raw, 0.0), axis=1, keepdims=True)
        table = jnp.where(lane == 4, peak, jnp.where(lane == 5, total, pick))
        cols[span, :] = jnp.where(lane == 0, old, table)
        return carry

    lax.fori_loop(0, half // step, measure_teacher, 0)
    for j, (low, size) in enumerate(chunks):
        arrived(landed.at[:, pl.ds(low, size)], halves[j])

    def measure_student(i, carry):
        span = pl.ds(pl.multiple_of(i * step, step), step)
        student = jnp.where(inside, logits[span, :] + landed[span, :], LOW)
        logits[span, :] = student
        raw = teach[span, :].astype(jnp.float32)
        old = cols[span, :]
        chosen = (column_f == old[:, 0:1] - base) & inside
        peak = jnp.max(student, axis=1, keepdims=True)
        exps = jnp.exp(student - peak)
        found = {
            1: peak,
            2: jnp.sum(exps, axis=1, keepdims=True),
            3: jnp.sum(exps * (student - raw), axis=1, keepdims=True),
            6: jnp.sum(jnp.where(chosen, student, 0.0), axis=1, keepdims=True),
        }
        for k, value in found.items():
            old = jnp.where(lane == k, value, old)
        cols[span, :] = old
        return carry

    lax.fori_loop(0, half // step, measure_student, 0)

    def pack(group, carry):
        table = jnp.transpose(cols[pl.ds(pl.multiple_of(group * rows, rows), rows), :])
        near[0, group] = table[0:8]
        return carry

    lax.fori_loop(0, NX, pack, 0)
    slots = [
        send(near.at[0], near.at[k + 1], device((x + dx) % NX, h, yl, z, (c + dc) % NC))
        for k, (dx, dc) in enumerate(PAIR_PEERS)
    ]
    for k, slot in enumerate(slots):
        arrived(near.at[k + 1], slot)
    for k, value in enumerate(merge(near[:, :, 1:8])):
        far[0, :, k] = value
    token_row = near[0, :, 0]
    far[0, :, 7] = token_row
    slots = [
        send(far.at[0], far.at[k + 1], device(x, h, (yl + dy) % NYL, (z + dz) % NZ, c))
        for k, (dy, dz) in enumerate(LINE_PEERS)
    ]
    for side in range(NH):
        for p in range(NX):
            start, spot = side * half + p * rows, p * 2 * rows + side * rows
            own[spot : spot + rows, :] = wide[
                start : start + rows, pl.ds(pl.multiple_of(x * depth, depth), depth)
            ]
    for k, slot in enumerate(slots):
        arrived(far.at[k + 1], slot)
    peak_s, sum_s, weighted, peak_t, sum_t, pick_s, pick_t = merge(far[...])

    total_rows = jnp.sum(metas[:, 1, 0:1])
    student_norm = peak_s + jnp.log(sum_s)
    teacher_norm = peak_t + jnp.log(sum_t)
    mean_gap = weighted / sum_s
    divergence = mean_gap - student_norm + teacher_norm
    advantage = (pick_t - teacher_norm) - (pick_s - student_norm)
    counts = jnp.stack([metas[group * 2 + h][1] for group in range(NX)], axis=0)
    valid = lax.broadcasted_iota(jnp.int32, (NX, rows), 1).astype(jnp.float32) < counts
    row_weight = jnp.where(valid, rows / total_rows, 0.0)
    kl = jnp.where(valid, divergence, 0.0)
    own_group = lax.broadcasted_iota(jnp.int32, (NX, rows), 0) == x
    kl_ref[...] = jnp.sum(jnp.where(own_group, kl, 0.0), axis=0, keepdims=True)
    table = [
        peak_s, 1.0 / sum_s, mean_gap, row_weight * KL_SCALE, row_weight * advantage, token_row,
        token_row, token_row,
    ]
    for k, value in enumerate(table):
        outcome[:, k] = value

    def place_of(xs, hs, p, low=0, size=None):
        start = pl.multiple_of(p * 2 * rows + hs * rows + low, step)
        return every.at[xs, pl.ds(start, rows if size is None else size), :]

    per = rows // step

    def finish(i, carry):
        span = pl.ds(pl.multiple_of(i * step, step), step)
        goal = pl.ds(pl.multiple_of((i // per * 2 + h) * rows + i % per * step, step), step)
        student = logits[span, :]
        raw = teach[span, :].astype(jnp.float32)
        table = cols[span, :]
        probs = jnp.exp(student - table[:, 0:1]) * table[:, 1:2]
        chosen = (column_f == table[:, 5:6] - base) & inside
        adv = table[:, 4:5]
        grad = probs * (table[:, 3:4] * ((student - raw) - table[:, 2:3]) + adv)
        grad = grad - jnp.where(chosen, adv, 0.0)
        every[x, goal, :] = grad.astype(jnp.bfloat16)
        return carry

    direct = []

    def spread_grad():
        if len(direct) < NX:
            spot = place_of(x, h, len(direct))
            direct.append([send(spot, spot, to_right), send(spot, spot, to_left), send(spot, spot, partner)])

    for p in range(NX):
        cols[p * rows : (p + 1) * rows, :] = to_columns(outcome[p])
        lax.fori_loop(p * per, (p + 1) * per, finish, 0)
        if p < 2:
            spread_grad()

    def rows_part(p):
        start = p * 2 * rows
        out = jnp.zeros((2 * rows, depth), jnp.float32)
        for xs in range(NX):
            out = out + jnp.dot(
                every[xs, start : start + 2 * rows, :],
                padded[xs * width : (xs + 1) * width, :],
                preferred_element_type=jnp.float32,
            )
        for side in range(NH):
            for s in range(4):
                rows_out[p, s % 2, s // 2, side] = out[
                    side * rows : (side + 1) * rows, s * TILE : (s + 1) * TILE
                ]
        return send(rows_out.at[p, 1 - c], paired.at[p], mate)

    lines = []

    def line_up(p, slot):
        arrived(paired.at[p], slot)
        for zt in range(NZ):
            span = pl.ds(zt % 4 * part, part)
            for b in range(NYL):
                staged[p, zt, b] = rows_out[p, c, b, zt // 4, span, :] + paired[p, b, zt // 4, span, :]
        lines.append(
            [
                send(
                    staged.at[p, (z + dz) % NZ], lined.at[p, dz], device(x, h, yl, (z + dz) % NZ, c)
                )
                for dz in range(1, NZ)
            ]
        )

    def deliver(p):
        for dz in range(1, NZ):
            arrived(lined.at[p, dz], lines[p][dz - 1])
        total = staged[p, z]
        for dz in range(1, NZ):
            total = total + lined[p, dz]
        cross_out[p] = total
        span = pl.ds(pl.multiple_of(quarter * part, part), part)
        for b in range(NYL):

            @pl.when(leaves[p, b])
            def _():
                pltpu.make_async_remote_copy(
                    src_ref=cross_out.at[p, b], dst_ref=final_in.at[yl, span, :],
                    send_sem=end_sent.at[p * NYL + b], recv_sem=end_got.at[yl * 4 + quarter],
                    device_id={"grp": goals[p, b][0], "vocab": goals[p, b][1]}, device_id_type=MESH,
                ).start()

            @pl.when(jnp.logical_not(leaves[p, b]))
            def _():
                final_in[yl, span, :] = cross_out[p, b]

    far_own, last, paired_slots = [], [], []
    for p in range(NX + 3):
        if p < NX:
            arrived(place_of(left, h, p), direct[p][0])
            lead = place_of(left, h, p, 0, step)
            a = send(lead, lead, to_right)
            arrived(place_of(right, h, p), direct[p][1])
            tail = place_of(right, h, p, step, step)
            far_own.append((a, send(tail, tail, to_left)))
            if p == NX - 1:
                lower = place_of(left, h, p, step, step)
                cross = [send(lower, lower, partner), send(tail, tail, partner)]
            spread_grad()
        if 1 <= p <= NX:
            q = p - 1
            arrived(place_of(opposite, h, q, 0, step), far_own[q][0])
            arrived(place_of(opposite, h, q, step, step), far_own[q][1])
            spot = place_of(opposite, h, q)
            far_half = send(spot, spot, partner)
            spot = place_of(x, 1 - h, q)
            arrived(spot, direct[q][2])
            if q == NX - 1:
                spot = place_of(x, 1 - h, q, 0, step)
            last.append([send(spot, spot, to_right), send(spot, spot, to_left), far_half])
        if 3 <= p:
            line_up(p - 3, paired_slots[p - 3])
        if 2 <= p <= NX + 1:
            q = p - 2
            size = rows
            if q == NX - 1:
                size = step
                arrived(place_of(left, 1 - h, q, step, step), cross[0])
                arrived(place_of(right, 1 - h, q, step, step), cross[1])
            arrived(place_of(left, 1 - h, q, 0, size), last[q][0])
            arrived(place_of(right, 1 - h, q, 0, size), last[q][1])
            arrived(place_of(opposite, 1 - h, q), last[q][2])
            paired_slots.append(rows_part(q))
    for p in range(NX - 2):
        deliver(p)

    for xs in range(NX):
        size = min(width, slab - xs * width)
        out = lax.dot_general(
            every[xs], own[...], (((0,), (0,)), ((), ())), preferred_element_type=jnp.float32
        )
        head_ref[xs * width : xs * width + size, :] = out[:size].astype(jnp.bfloat16)
    for p in (NX - 2, NX - 1):
        deliver(p)
    for b, k in origins:

        @pl.when(comes[b, k])
        def _():
            spot = final_in.at[b, pl.ds(k * part, part), :]
            pltpu.make_async_copy(spot, spot, end_got.at[b * 4 + k]).wait()

    out_ref[...] = (final_in[0] + final_in[1]).astype(jnp.bfloat16)
    for p, b in goals:

        @pl.when(leaves[p, b])
        def _():
            spot = cross_out.at[p, b]
            pltpu.make_async_copy(spot, spot, end_sent.at[p * NYL + b]).wait()

    for copy in pending:
        copy.wait_send()


def write_kernel(*refs):
    count = len(refs) // 2
    for k in range(count):
        refs[count + k][...] = refs[k][...]


def shards(hidden, weight, teacher_panels, token_ids, row_counts):
    rows = hidden.shape[0]
    depth, slab = weight.shape
    width = -(-slab // (NX * TILE)) * TILE
    half, tokens = NX * rows, NX * NH * rows
    chunks = tuple((low, TILE) for low in range(0, width, TILE))
    m, q = len(PAIR_PEERS), len(LINE_PEERS)
    part = rows * NH // NZ
    vmem = pl.BlockSpec(memory_space=pltpu.VMEM)
    f32, bf16 = jnp.float32, jnp.bfloat16
    copies = 5 * len(GROUP_PEERS) + 4 * len(chunks) + 2 * m + q + (9 + NZ - 1) * NX + 2
    head_grad, hidden_grad, kl = pl.pallas_call(
        functools.partial(fused_kernel, slab, chunks),
        name="distill",
        out_shape=[
            jax.ShapeDtypeStruct((slab, depth), bf16),
            jax.ShapeDtypeStruct((rows, TILE), bf16),
            jax.ShapeDtypeStruct((1, rows), f32),
        ],
        in_specs=[vmem] * 4 + [pl.BlockSpec(memory_space=pltpu.SMEM)],
        out_specs=[vmem] * 3,
        scratch_shapes=[
            pltpu.VMEM((NX * width, depth), bf16),
            pltpu.VMEM((tokens, NX * depth), bf16),
            pltpu.VMEM((width, NX * depth), bf16),
            pltpu.VMEM((half, width), f32),
            pltpu.VMEM((half, width), f32),
            pltpu.VMEM((half, width), f32),
            pltpu.VMEM((NC, rows // 2, NX * width), bf16),
            pltpu.VMEM((half, width), bf16),
            pltpu.VMEM((8, rows), f32),
            pltpu.VMEM((NX * NH, 8, rows), f32),
            pltpu.VMEM((m + 1, NX, 8, rows), f32),
            pltpu.VMEM((q + 1, NX, 8, rows), f32),
            pltpu.VMEM((NX, 8, rows), f32),
            pltpu.VMEM((half, TILE), f32),
            pltpu.VMEM((NX, tokens, width), bf16),
            pltpu.VMEM((tokens, depth), bf16),
            pltpu.VMEM((NX, NC, NYL, NH, rows, TILE), f32),
            pltpu.VMEM((NX, NYL, NH, rows, TILE), f32),
            pltpu.VMEM((NX, NZ, NYL, part, TILE), f32),
            pltpu.VMEM((NX, NZ, NYL, part, TILE), f32),
            pltpu.VMEM((NX, NYL, part, TILE), f32),
            pltpu.VMEM((NYL, rows, TILE), f32),
            pltpu.SemaphoreType.DMA((NX + 1,)),
            pltpu.SemaphoreType.DMA((copies,)),
            pltpu.SemaphoreType.DMA((copies,)),
            pltpu.SemaphoreType.DMA((NX * NYL,)),
            pltpu.SemaphoreType.DMA((NYL * 4,)),
        ],
        compiler_params=pltpu.CompilerParams(
            collective_id=1, has_side_effects=True, vmem_limit_bytes=56 * 2**20
        ),
    )(hidden, weight.T, teacher_panels, token_ids[None], row_counts)
    results = (head_grad, hidden_grad, kl)
    head_grad, hidden_grad, kl = pl.pallas_call(
        write_kernel,
        name="write",
        out_shape=[jax.ShapeDtypeStruct(r.shape, r.dtype) for r in results],
        in_specs=[vmem] * 3,
        out_specs=[vmem] * 3,
    )(*results)
    return kl[0], hidden_grad, head_grad.T


def solution(mesh):
    return jax.shard_map(
        shards,
        mesh=mesh,
        in_specs=(P("grp", None), P("grp", "vocab"), P("grp", "vocab"), P("grp"), P("grp")),
        out_specs=(P("grp"), P("grp", "vocab"), P("grp", "vocab")),
        check_vma=False,
    )
```

```python
import functools

import jax
import jax.numpy as jnp
from jax import lax
from jax.experimental import pallas as pl
from jax.experimental.pallas import tpu as pltpu
from jax.sharding import PartitionSpec as P

KL_SCALE = 256.0
MESH = pl.DeviceIdType.MESH
LOW = -1e30
NX, NH, NYL, NZ, NC = 4, 2, 2, 8, 2
TILE = 128
GROUP_PEERS = [(dx, dh) for dh in (1, 0) for dx in (0, 1, 3, 2) if dx or dh]
PAIR_PEERS = [(dx, dc) for dc in (0, 1) for dx in (1, 3, 2, 0) if dx or dc]
LINE_PEERS = [(dy, dz) for dy in (0, 1) for dz in range(NZ) if dy or dz]


def place():
    g = lax.axis_index("grp")
    v = lax.axis_index("vocab")
    return g // 2, g % 2, v // 16, (v // 2) % 8, v % 2


def device(x, h, yl, z, c):
    return {"grp": x * 2 + h, "vocab": yl * 16 + z * 2 + c}


def to_columns(tile):
    return jnp.transpose(jnp.concatenate([tile] * (TILE // 8), axis=0))


def merge(buf):
    peak_s = jnp.max(buf[:, :, 0], axis=0)
    scale_s = jnp.exp(buf[:, :, 0] - peak_s[None])
    peak_t = jnp.max(buf[:, :, 3], axis=0)
    scale_t = jnp.exp(buf[:, :, 3] - peak_t[None])
    return [
        peak_s,
        jnp.sum(buf[:, :, 1] * scale_s, axis=0),
        jnp.sum(buf[:, :, 2] * scale_s, axis=0),
        peak_t,
        jnp.sum(buf[:, :, 4] * scale_t, axis=0),
        jnp.sum(buf[:, :, 5], axis=0),
        jnp.sum(buf[:, :, 6], axis=0),
    ]


def fused_kernel(
    slab,
    chunks,
    hidden_hbm,
    weight_hbm,
    panel_hbm,
    token_ref,
    count_ref,
    head_hbm,
    out_ref,
    kl_ref,
    hidden_ref,
    weight_ref,
    panel_ref,
    padded,
    wide,
    heads,
    partial,
    landed,
    logits,
    teacher,
    teach,
    meta,
    metas,
    near,
    far,
    merged,
    outcome,
    cols,
    every,
    own,
    rows_out,
    paired,
    staged,
    lined,
    cross_out,
    final_in,
    local_sem,
    sent,
    got,
    end_sent,
    end_got,
):
    x, h, yl, z, c = place()
    rows, depth = hidden_ref.shape[0], padded.shape[1]
    above = GROUP_PEERS[:NX]
    beside = GROUP_PEERS[NX:]
    half = NX * rows
    width = padded.shape[0] // NX
    z_pair = z + 1 - 2 * lax.rem(z, 2)
    g = x * 2 + h
    v = yl * 16 + z * 2 + c
    part = rows * NH // NZ
    quarter = lax.rem(z, 4)
    goals = {(p, b): (2 * p + z // 4, 4 * g + 2 * b + c) for p in range(NX) for b in range(NYL)}
    origins = {
        (b, k): (v // 4, b * 16 + ((g % 2) * 4 + k) * 2 + v % 2) for b in range(NYL) for k in range(4)
    }
    leaves = {key: (a != g) | (b != v) for key, (a, b) in goals.items()}
    comes = {key: (a != g) | (b != v) for key, (a, b) in origins.items()}
    partner = device(x, 1 - h, yl, z, c)
    mate = device(x, h, yl, z, 1 - c)
    right, left = (x + 1) % NX, (x + NX - 1) % NX
    opposite = (x + 2) % NX
    to_right, to_left = device(right, h, yl, z, c), device(left, h, yl, z, c)

    loads = [
        pltpu.make_async_copy(hidden_hbm, hidden_ref, local_sem.at[NX + 1]),
        pltpu.make_async_copy(weight_hbm, weight_ref, local_sem.at[NX + 2]),
        pltpu.make_async_copy(panel_hbm, panel_ref, local_sem.at[NX + 3]),
    ]
    for load in loads:
        load.start()
    barrier = pltpu.get_barrier_semaphore()
    peers = [device((x + dx) % NX, (h + dh) % NH, yl, z, c) for dx, dh in GROUP_PEERS]
    peers += [device((x + dx) % NX, h, yl, z, 1 - c) for dx in range(NX)]
    peers += [device(x, h, (yl + dy) % NYL, (z + dz) % NZ, c) for dy, dz in LINE_PEERS]
    for peer in peers:
        pl.semaphore_signal(barrier, inc=1, device_id=peer, device_id_type=MESH)

    for key, (a, b) in origins.items():

        @pl.when(comes[key])
        def _():
            pl.semaphore_signal(
                barrier, inc=1, device_id={"grp": a, "vocab": b}, device_id_type=MESH
            )

    meta[...] = jnp.where(
        lax.broadcasted_iota(jnp.int32, meta.shape, 0) == 0,
        token_ref[...].astype(jnp.float32),
        count_ref[0].astype(jnp.float32),
    )
    metas[g] = meta[...]
    loads[0].wait()
    loads[1].wait()
    padded[0:slab, :] = weight_ref[...]
    padded[slab:, :] = jnp.zeros((NX * width - slab, depth), padded.dtype)
    others = sum(jnp.where(leave, 1, 0) for leave in leaves.values())
    pl.semaphore_wait(barrier, len(peers) + others)

    pending = []

    def send(src, dst, target):
        slot = len(pending)
        copy = pltpu.make_async_remote_copy(
            src_ref=src, dst_ref=dst, send_sem=sent.at[slot], recv_sem=got.at[slot],
            device_id=target, device_id_type=MESH,
        )
        copy.start()
        pending.append(copy)
        return slot

    def arrived(ref, slot):
        pltpu.make_async_copy(ref, ref, got.at[slot]).wait()

    parity = lax.rem(z, 2)
    mine, other = 2 * c + parity, 2 * c + 1 - parity

    def region(xs, hs, kx):
        return wide.at[
            pl.ds(pl.multiple_of(hs * half + xs * rows, rows), rows),
            pl.ds(pl.multiple_of(kx * depth, depth), depth),
        ]

    def block(kx, hs):
        return hidden_ref.at[:, pl.ds(pl.multiple_of((kx * 2 + hs) * depth, depth), depth)]

    hid = {}

    def spread(peers):
        for dx, dh in peers:
            xt, ht = (x + dx) % NX, (h + dh) % NH
            hid[dx, dh] = send(block(mine, ht), region(x, h, mine), device(xt, ht, yl, z, c))

    def weight_rows(xs, low, size):
        return pl.ds(pl.multiple_of(xs * width + low, TILE), size)

    def head_spot(kx, low, size):
        return heads.at[pl.ds(low, size), pl.ds(pl.multiple_of(kx * depth, depth), depth)]

    wgt = []

    def spread_weight():
        if len(wgt) < len(chunks):
            low, size = chunks[len(wgt)]
            wgt.append(
                [
                    send(
                        padded.at[weight_rows((x + dx) % NX, low, size), :],
                        head_spot(x, low, size),
                        device((x + dx) % NX, h, yl, z, c),
                    )
                    for dx in (1, 3, 2)
                ]
            )

    fwd, near_core, far_core, met = {}, {}, {}, {}

    def source(peer):
        return (x - peer[0] + NX) % NX, (h + peer[1]) % NH

    def pass_on(peers):
        for peer in peers:
            spot = region(*source(peer), mine)
            arrived(spot, hid[peer])
            fwd[peer] = send(spot, spot, device(x, h, yl, z_pair, c))
            near_core[peer] = send(spot, spot, mate)

    def pass_core(peers):
        for peer in peers:
            spot = region(*source(peer), other)
            arrived(spot, fwd[peer])
            far_core[peer] = send(spot, spot, mate)

    def collect(peers):
        for peer in peers:
            xs, hs = source(peer)
            arrived(region(xs, hs, 2 * (1 - c) + parity), near_core[peer])
            arrived(region(xs, hs, 2 * (1 - c) + 1 - parity), far_core[peer])

    spread(above)
    spread_weight()
    spread_weight()
    for dx, dh in GROUP_PEERS:
        met[dx, dh] = send(meta, metas.at[g], device((x + dx) % NX, (h + dh) % NH, yl, z, c))
    locals_ = [
        pltpu.make_async_copy(block(kx, h), region(x, h, kx), local_sem.at[kx]) for kx in range(NX)
    ]
    locals_.append(
        pltpu.make_async_copy(
            padded.at[weight_rows(x, 0, width), :], head_spot(x, 0, width), local_sem.at[NX]
        )
    )
    for copy in locals_:
        copy.start()

    loads[2].wait()
    teacher[...] = jnp.zeros_like(teacher)
    for side in range(NC):
        teacher[side, :, 0:slab] = panel_ref[:, side * slab : (side + 1) * slab]

    pass_on(above)
    spread_weight()
    pass_core(above)
    spread(beside)
    spread_weight()
    for copy in locals_:
        copy.wait()
    for peer in GROUP_PEERS:
        xs, hs = source(peer)
        arrived(metas.at[xs * 2 + hs], met[peer])
    collect(above)

    def product(side, low, size):
        return lax.dot_general(
            wide[pl.ds(pl.multiple_of(side * half, half), half), :],
            heads[low : low + size, :],
            (((1,), (1,)), ((), ())),
            preferred_element_type=jnp.float32,
        )

    def teach_spot(xs, cs):
        step = rows // 2
        return teach.at[pl.ds(pl.multiple_of(xs * rows + cs * step, step), step), :]

    def teacher_piece(xt, ct):
        return teacher.at[ct, :, pl.ds(pl.multiple_of(xt * width, TILE), width)]

    halves, teaching = [], []
    for j, (low, size) in enumerate(chunks):
        for k, dx in enumerate((1, 3, 2)):
            arrived(head_spot((x - dx + NX) % NX, low, size), wgt[j][k])
        partial[:, low : low + size] = product(1 - h, low, size)
        piece = pl.ds(low, size)
        halves.append(send(partial.at[:, piece], landed.at[:, piece], partner))
        spread_weight()
        if j == 1:
            pass_on(beside)
        if j == 2:
            pass_core(beside)
        if j == len(chunks) - 2:
            keep = pltpu.make_async_copy(teacher_piece(x, c), teach_spot(x, c), local_sem.at[0])
            keep.start()
            for dx, dc in PAIR_PEERS:
                xt, ct = (x + dx) % NX, (c + dc) % NC
                teaching.append(send(teacher_piece(xt, ct), teach_spot(x, c), device(xt, h, yl, z, ct)))
    collect(beside)
    for low in range(0, width, 256):
        size = min(256, width - low)
        logits[:, low : low + size] = product(h, low, size)

    step = rows // 2
    lane = lax.broadcasted_iota(jnp.int32, (step, TILE), 1)
    column = lax.broadcasted_iota(jnp.int32, (step, width), 1)
    inside = column < slab - x * width
    base = (v * slab + x * width).astype(jnp.float32)
    column_f = column.astype(jnp.float32)

    def fill(group, carry):
        cols[pl.ds(pl.multiple_of(group * rows, rows), rows), :] = to_columns(metas[group * 2 + h])
        return carry

    lax.fori_loop(0, NX, fill, 0)
    keep.wait()
    for k, (dx, dc) in enumerate(PAIR_PEERS):
        arrived(teach_spot((x - dx + NX) % NX, (c + dc) % NC), teaching[k])

    def measure_teacher(i, carry):
        span = pl.ds(pl.multiple_of(i * step, step), step)
        raw = teach[span, :].astype(jnp.float32)
        masked = jnp.where(inside, raw, LOW)
        old = cols[span, :]
        chosen = (column_f == old[:, 0:1] - base) & inside
        peak = jnp.max(masked, axis=1, keepdims=True)
        total = jnp.sum(jnp.exp(masked - peak), axis=1, keepdims=True)
        pick = jnp.sum(jnp.where(chosen, raw, 0.0), axis=1, keepdims=True)
        table = jnp.where(lane == 4, peak, jnp.where(lane == 5, total, pick))
        cols[span, :] = jnp.where(lane == 0, old, table)
        return carry

    lax.fori_loop(0, half // step, measure_teacher, 0)
    for j, (low, size) in enumerate(chunks):
        arrived(landed.at[:, pl.ds(low, size)], halves[j])

    def measure_student(i, carry):
        span = pl.ds(pl.multiple_of(i * step, step), step)
        student = jnp.where(inside, logits[span, :] + landed[span, :], LOW)
        logits[span, :] = student
        raw = teach[span, :].astype(jnp.float32)
        old = cols[span, :]
        chosen = (column_f == old[:, 0:1] - base) & inside
        peak = jnp.max(student, axis=1, keepdims=True)
        exps = jnp.exp(student - peak)
        found = {
            1: peak,
            2: jnp.sum(exps, axis=1, keepdims=True),
            3: jnp.sum(exps * (student - raw), axis=1, keepdims=True),
            6: jnp.sum(jnp.where(chosen, student, 0.0), axis=1, keepdims=True),
        }
        for k, value in found.items():
            old = jnp.where(lane == k, value, old)
        cols[span, :] = old
        return carry

    lax.fori_loop(0, half // step, measure_student, 0)

    def pack(group, carry):
        table = jnp.transpose(cols[pl.ds(pl.multiple_of(group * rows, rows), rows), :])
        near[0, group] = table[0:8]
        return carry

    lax.fori_loop(0, NX, pack, 0)
    slots = [
        send(near.at[0], near.at[k + 1], device((x + dx) % NX, h, yl, z, (c + dc) % NC))
        for k, (dx, dc) in enumerate(PAIR_PEERS)
    ]
    for k, slot in enumerate(slots):
        arrived(near.at[k + 1], slot)
    for k, value in enumerate(merge(near[:, :, 1:8])):
        merged[:, k] = value
    merged[:, 7] = near[0, :, 0]
    pair = pl.ds(2 * c, 2)
    slots = [
        send(merged.at[pair], far.at[k + 1], device(x, h, (yl + dy) % NYL, (z + dz) % NZ, c))
        for k, (dy, dz) in enumerate(LINE_PEERS)
    ]
    far[0] = merged[pair]
    for side in range(NH):
        for p in range(NX):
            start, spot = side * half + p * rows, p * 2 * rows + side * rows
            own[spot : spot + rows, :] = wide[
                start : start + rows, pl.ds(pl.multiple_of(x * depth, depth), depth)
            ]
    for k, slot in enumerate(slots):
        arrived(far.at[k + 1], slot)
    peak_s, sum_s, weighted, peak_t, sum_t, pick_s, pick_t = merge(far[...])

    total_rows = jnp.sum(metas[:, 1, 0:1])
    student_norm = peak_s + jnp.log(sum_s)
    teacher_norm = peak_t + jnp.log(sum_t)
    mean_gap = weighted / sum_s
    divergence = mean_gap - student_norm + teacher_norm
    advantage = (pick_t - teacher_norm) - (pick_s - student_norm)
    counts = jnp.stack([metas[(2 * c + k) * 2 + h][1] for k in range(2)], axis=0)
    valid = lax.broadcasted_iota(jnp.int32, (2, rows), 1).astype(jnp.float32) < counts
    row_weight = jnp.where(valid, rows / total_rows, 0.0)
    kl = jnp.where(valid, divergence, 0.0)
    token_row = far[0, :, 7]
    table = [
        peak_s, 1.0 / sum_s, mean_gap, row_weight * KL_SCALE, row_weight * advantage, token_row, kl, kl,
    ]
    for k, value in enumerate(table):
        outcome[pair, k] = value
    slot = send(outcome.at[pair], outcome.at[pair], mate)
    arrived(outcome.at[pl.ds(2 - 2 * c, 2)], slot)
    kl_ref[...] = outcome[x, 6:7]

    def place_of(xs, hs, p, low=0, size=None):
        start = pl.multiple_of(p * 2 * rows + hs * rows + low, step)
        return every.at[xs, pl.ds(start, rows if size is None else size), :]

    per = rows // step

    def finish(i, carry):
        span = pl.ds(pl.multiple_of(i * step, step), step)
        goal = pl.ds(pl.multiple_of((i // per * 2 + h) * rows + i % per * step, step), step)
        student = logits[span, :]
        raw = teach[span, :].astype(jnp.float32)
        table = cols[span, :]
        probs = jnp.exp(student - table[:, 0:1]) * table[:, 1:2]
        chosen = (column_f == table[:, 5:6] - base) & inside
        adv = table[:, 4:5]
        grad = probs * (table[:, 3:4] * ((student - raw) - table[:, 2:3]) + adv)
        grad = grad - jnp.where(chosen, adv, 0.0)
        every[x, goal, :] = grad.astype(jnp.bfloat16)
        return carry

    direct = []

    def spread_grad():
        if len(direct) < NX:
            spot = place_of(x, h, len(direct))
            direct.append([send(spot, spot, to_right), send(spot, spot, to_left), send(spot, spot, partner)])

    for p in range(NX):
        cols[p * rows : (p + 1) * rows, :] = to_columns(outcome[p])
        lax.fori_loop(p * per, (p + 1) * per, finish, 0)
        if p < 2:
            spread_grad()

    def rows_part(p):
        start = p * 2 * rows
        out = jnp.zeros((2 * rows, depth), jnp.float32)
        for xs in range(NX):
            out = out + jnp.dot(
                every[xs, start : start + 2 * rows, :],
                padded[xs * width : (xs + 1) * width, :],
                preferred_element_type=jnp.float32,
            )
        for side in range(NH):
            for s in range(4):
                rows_out[p, s % 2, s // 2, side] = out[
                    side * rows : (side + 1) * rows, s * TILE : (s + 1) * TILE
                ]
        return send(rows_out.at[p, 1 - c], paired.at[p], mate)

    lines = []

    def line_up(p, slot):
        arrived(paired.at[p], slot)
        for zt in range(NZ):
            span = pl.ds(zt % 4 * part, part)
            for b in range(NYL):
                staged[p, zt, b] = rows_out[p, c, b, zt // 4, span, :] + paired[p, b, zt // 4, span, :]
        lines.append(
            [
                send(
                    staged.at[p, (z + dz) % NZ], lined.at[p, dz], device(x, h, yl, (z + dz) % NZ, c)
                )
                for dz in range(1, NZ)
            ]
        )

    def deliver(p):
        for dz in range(1, NZ):
            arrived(lined.at[p, dz], lines[p][dz - 1])
        total = staged[p, z]
        for dz in range(1, NZ):
            total = total + lined[p, dz]
        cross_out[p] = total
        span = pl.ds(pl.multiple_of(quarter * part, part), part)
        for b in range(NYL):

            @pl.when(leaves[p, b])
            def _():
                pltpu.make_async_remote_copy(
                    src_ref=cross_out.at[p, b], dst_ref=final_in.at[yl, span, :],
                    send_sem=end_sent.at[p * NYL + b], recv_sem=end_got.at[yl * 4 + quarter],
                    device_id={"grp": goals[p, b][0], "vocab": goals[p, b][1]}, device_id_type=MESH,
                ).start()

            @pl.when(jnp.logical_not(leaves[p, b]))
            def _():
                final_in[yl, span, :] = cross_out[p, b]

    far_own, last, paired_slots = [], [], []
    for p in range(NX + 3):
        if p < NX:
            arrived(place_of(left, h, p), direct[p][0])
            lead = place_of(left, h, p, 0, step)
            a = send(lead, lead, to_right)
            arrived(place_of(right, h, p), direct[p][1])
            tail = place_of(right, h, p, step, step)
            far_own.append((a, send(tail, tail, to_left)))
            if p == NX - 1:
                lower = place_of(left, h, p, step, step)
                cross = [send(lower, lower, partner), send(tail, tail, partner)]
            spread_grad()
        if 1 <= p <= NX:
            q = p - 1
            arrived(place_of(opposite, h, q, 0, step), far_own[q][0])
            arrived(place_of(opposite, h, q, step, step), far_own[q][1])
            spot = place_of(opposite, h, q)
            far_half = send(spot, spot, partner)
            spot = place_of(x, 1 - h, q)
            arrived(spot, direct[q][2])
            if q == NX - 1:
                spot = place_of(x, 1 - h, q, 0, step)
            last.append([send(spot, spot, to_right), send(spot, spot, to_left), far_half])
        if 3 <= p:
            line_up(p - 3, paired_slots[p - 3])
        if 2 <= p <= NX + 1:
            q = p - 2
            size = rows
            if q == NX - 1:
                size = step
                arrived(place_of(left, 1 - h, q, step, step), cross[0])
                arrived(place_of(right, 1 - h, q, step, step), cross[1])
            arrived(place_of(left, 1 - h, q, 0, size), last[q][0])
            arrived(place_of(right, 1 - h, q, 0, size), last[q][1])
            arrived(place_of(opposite, 1 - h, q), last[q][2])
            paired_slots.append(rows_part(q))
    for p in range(NX - 2):
        deliver(p)

    for xs in range(NX):
        size = min(width, slab - xs * width)
        out = lax.dot_general(
            every[xs], own[...], (((0,), (0,)), ((), ())), preferred_element_type=jnp.float32
        )
        weight_ref[xs * width : xs * width + size, :] = out[:size].astype(jnp.bfloat16)
    store = pltpu.make_async_copy(weight_ref, head_hbm, local_sem.at[NX + 2])
    store.start()
    for p in (NX - 2, NX - 1):
        deliver(p)
    for b, k in origins:

        @pl.when(comes[b, k])
        def _():
            spot = final_in.at[b, pl.ds(k * part, part), :]
            pltpu.make_async_copy(spot, spot, end_got.at[b * 4 + k]).wait()

    out_ref[...] = (final_in[0] + final_in[1]).astype(jnp.bfloat16)
    for p, b in goals:

        @pl.when(leaves[p, b])
        def _():
            spot = cross_out.at[p, b]
            pltpu.make_async_copy(spot, spot, end_sent.at[p * NYL + b]).wait()

    for copy in pending:
        copy.wait_send()
    store.wait()


def write_kernel(*refs):
    count = len(refs) // 2
    for k in range(count):
        refs[count + k][...] = refs[k][...]


def shards(hidden, weight, teacher_panels, token_ids, row_counts):
    rows = hidden.shape[0]
    depth, slab = weight.shape
    width = -(-slab // (NX * TILE)) * TILE
    half, tokens = NX * rows, NX * NH * rows
    chunks = tuple((low, TILE) for low in range(0, width, TILE))
    m, q = len(PAIR_PEERS), len(LINE_PEERS)
    part = rows * NH // NZ
    vmem = pl.BlockSpec(memory_space=pltpu.VMEM)
    hbm = pl.BlockSpec(memory_space=pl.ANY)
    f32, bf16 = jnp.float32, jnp.bfloat16
    copies = 5 * len(GROUP_PEERS) + 4 * len(chunks) + 2 * m + q + (9 + NZ - 1) * NX + 3
    head_grad, hidden_grad, kl = pl.pallas_call(
        functools.partial(fused_kernel, slab, chunks),
        name="distill",
        out_shape=[
            jax.ShapeDtypeStruct((slab, depth), bf16),
            jax.ShapeDtypeStruct((rows, TILE), bf16),
            jax.ShapeDtypeStruct((1, rows), f32),
        ],
        in_specs=[hbm] * 3 + [vmem, pl.BlockSpec(memory_space=pltpu.SMEM)],
        out_specs=[hbm, vmem, vmem],
        scratch_shapes=[
            pltpu.VMEM(hidden.shape, bf16),
            pltpu.VMEM((slab, depth), bf16),
            pltpu.VMEM(teacher_panels.shape, bf16),
            pltpu.VMEM((NX * width, depth), bf16),
            pltpu.VMEM((tokens, NX * depth), bf16),
            pltpu.VMEM((width, NX * depth), bf16),
            pltpu.VMEM((half, width), f32),
            pltpu.VMEM((half, width), f32),
            pltpu.VMEM((half, width), f32),
            pltpu.VMEM((NC, rows // 2, NX * width), bf16),
            pltpu.VMEM((half, width), bf16),
            pltpu.VMEM((8, rows), f32),
            pltpu.VMEM((NX * NH, 8, rows), f32),
            pltpu.VMEM((m + 1, NX, 8, rows), f32),
            pltpu.VMEM((q + 1, 2, 8, rows), f32),
            pltpu.VMEM((NX, 8, rows), f32),
            pltpu.VMEM((NX, 8, rows), f32),
            pltpu.VMEM((half, TILE), f32),
            pltpu.VMEM((NX, tokens, width), bf16),
            pltpu.VMEM((tokens, depth), bf16),
            pltpu.VMEM((NX, NC, NYL, NH, rows, TILE), f32),
            pltpu.VMEM((NX, NYL, NH, rows, TILE), f32),
            pltpu.VMEM((NX, NZ, NYL, part, TILE), f32),
            pltpu.VMEM((NX, NZ, NYL, part, TILE), f32),
            pltpu.VMEM((NX, NYL, part, TILE), f32),
            pltpu.VMEM((NYL, rows, TILE), f32),
            pltpu.SemaphoreType.DMA((NX + 4,)),
            pltpu.SemaphoreType.DMA((copies,)),
            pltpu.SemaphoreType.DMA((copies,)),
            pltpu.SemaphoreType.DMA((NX * NYL,)),
            pltpu.SemaphoreType.DMA((NYL * 4,)),
        ],
        compiler_params=pltpu.CompilerParams(
            collective_id=1, has_side_effects=True, vmem_limit_bytes=56 * 2**20
        ),
    )(hidden, weight.T, teacher_panels, token_ids[None], row_counts)
    results = (head_grad, hidden_grad, kl)
    head_grad, hidden_grad, kl = pl.pallas_call(
        write_kernel,
        name="write",
        out_shape=[jax.ShapeDtypeStruct(r.shape, r.dtype) for r in results],
        in_specs=[vmem] * 3,
        out_specs=[vmem] * 3,
    )(*results)
    return kl[0], hidden_grad, head_grad.T


def solution(mesh):
    return jax.shard_map(
        shards,
        mesh=mesh,
        in_specs=(P("grp", None), P("grp", "vocab"), P("grp", "vocab"), P("grp"), P("grp")),
        out_specs=(P("grp"), P("grp", "vocab"), P("grp", "vocab")),
        check_vma=False,
    )
```

```python
import functools

import jax
import jax.numpy as jnp
from jax import lax
from jax.experimental import pallas as pl
from jax.experimental.pallas import tpu as pltpu
from jax.sharding import PartitionSpec as P

KL_SCALE = 256.0
MESH = pl.DeviceIdType.MESH
LOW = -1e30
NX, NH, NYL, NZ, NC = 4, 2, 2, 8, 2
TILE = 128
GROUP_PEERS = [(dx, dh) for dh in (1, 0) for dx in (0, 1, 3, 2) if dx or dh]
PAIR_PEERS = [(dx, dc) for dc in (0, 1) for dx in (1, 3, 2, 0) if dx or dc]
LINE_PEERS = [(dy, dz) for dy in (0, 1) for dz in range(NZ) if dy or dz]


def place():
    g = lax.axis_index("grp")
    v = lax.axis_index("vocab")
    return g // 2, g % 2, v // 16, (v // 2) % 8, v % 2


def device(x, h, yl, z, c):
    return {"grp": x * 2 + h, "vocab": yl * 16 + z * 2 + c}


def to_columns(tile):
    return jnp.transpose(jnp.concatenate([tile] * (TILE // 8), axis=0))


def merge(buf):
    peak_s = jnp.max(buf[:, :, 0], axis=0)
    scale_s = jnp.exp(buf[:, :, 0] - peak_s[None])
    peak_t = jnp.max(buf[:, :, 3], axis=0)
    scale_t = jnp.exp(buf[:, :, 3] - peak_t[None])
    return [
        peak_s,
        jnp.sum(buf[:, :, 1] * scale_s, axis=0),
        jnp.sum(buf[:, :, 2] * scale_s, axis=0),
        peak_t,
        jnp.sum(buf[:, :, 4] * scale_t, axis=0),
        jnp.sum(buf[:, :, 5], axis=0),
        jnp.sum(buf[:, :, 6], axis=0),
    ]


def fused_kernel(
    slab,
    chunks,
    hidden_hbm,
    weight_hbm,
    panel_hbm,
    tail_ref,
    token_ref,
    count_ref,
    head_hbm,
    out_ref,
    kl_ref,
    hidden_ref,
    head_ref,
    panel_ref,
    padded,
    wide,
    heads,
    partial,
    landed,
    logits,
    teacher,
    teach,
    meta,
    metas,
    near,
    far,
    merged,
    outcome,
    cols,
    every,
    own,
    rows_out,
    paired,
    staged,
    lined,
    cross_out,
    final_in,
    local_sem,
    sent,
    got,
    end_sent,
    end_got,
):
    x, h, yl, z, c = place()
    rows, depth = hidden_ref.shape[0], padded.shape[1]
    above = GROUP_PEERS[:NX]
    beside = GROUP_PEERS[NX:]
    half = NX * rows
    width = padded.shape[0] // NX
    z_pair = z + 1 - 2 * lax.rem(z, 2)
    g = x * 2 + h
    v = yl * 16 + z * 2 + c
    part = rows * NH // NZ
    quarter = lax.rem(z, 4)
    goals = {(p, b): (2 * p + z // 4, 4 * g + 2 * b + c) for p in range(NX) for b in range(NYL)}
    origins = {
        (b, k): (v // 4, b * 16 + ((g % 2) * 4 + k) * 2 + v % 2) for b in range(NYL) for k in range(4)
    }
    leaves = {key: (a != g) | (b != v) for key, (a, b) in goals.items()}
    comes = {key: (a != g) | (b != v) for key, (a, b) in origins.items()}
    partner = device(x, 1 - h, yl, z, c)
    mate = device(x, h, yl, z, 1 - c)
    right, left = (x + 1) % NX, (x + NX - 1) % NX
    opposite = (x + 2) % NX
    to_right, to_left = device(right, h, yl, z, c), device(left, h, yl, z, c)

    whole = slab // 16 * 16
    loads = [
        pltpu.make_async_copy(hidden_hbm, hidden_ref, local_sem.at[NX + 1]),
        pltpu.make_async_copy(
            weight_hbm.at[pl.ds(0, whole)], padded.at[pl.ds(0, whole)], local_sem.at[NX + 2]
        ),
        pltpu.make_async_copy(panel_hbm, panel_ref, local_sem.at[NX + 3]),
    ]
    for load in loads:
        load.start()
    barrier = pltpu.get_barrier_semaphore()
    peers = [device((x + dx) % NX, (h + dh) % NH, yl, z, c) for dx, dh in GROUP_PEERS]
    peers += [device((x + dx) % NX, h, yl, z, 1 - c) for dx in range(NX)]
    peers += [device(x, h, (yl + dy) % NYL, (z + dz) % NZ, c) for dy, dz in LINE_PEERS]
    for peer in peers:
        pl.semaphore_signal(barrier, inc=1, device_id=peer, device_id_type=MESH)

    for key, (a, b) in origins.items():

        @pl.when(comes[key])
        def _():
            pl.semaphore_signal(
                barrier, inc=1, device_id={"grp": a, "vocab": b}, device_id_type=MESH
            )

    meta[...] = jnp.where(
        lax.broadcasted_iota(jnp.int32, meta.shape, 0) == 0,
        token_ref[...].astype(jnp.float32),
        count_ref[0].astype(jnp.float32),
    )
    metas[g] = meta[...]
    padded[whole : whole + 16, :] = tail_ref[...]
    padded[whole + 16 :, :] = jnp.zeros((NX * width - whole - 16, depth), padded.dtype)
    loads[0].wait()
    loads[1].wait()
    others = sum(jnp.where(leave, 1, 0) for leave in leaves.values())
    pl.semaphore_wait(barrier, len(peers) + others)

    pending = []

    def send(src, dst, target):
        slot = len(pending)
        copy = pltpu.make_async_remote_copy(
            src_ref=src, dst_ref=dst, send_sem=sent.at[slot], recv_sem=got.at[slot],
            device_id=target, device_id_type=MESH,
        )
        copy.start()
        pending.append(copy)
        return slot

    def arrived(ref, slot):
        pltpu.make_async_copy(ref, ref, got.at[slot]).wait()

    parity = lax.rem(z, 2)
    mine, other = 2 * c + parity, 2 * c + 1 - parity

    def region(xs, hs, kx):
        return wide.at[
            pl.ds(pl.multiple_of(hs * half + xs * rows, rows), rows),
            pl.ds(pl.multiple_of(kx * depth, depth), depth),
        ]

    def block(kx, hs):
        return hidden_ref.at[:, pl.ds(pl.multiple_of((kx * 2 + hs) * depth, depth), depth)]

    hid = {}

    def spread(peers):
        for dx, dh in peers:
            xt, ht = (x + dx) % NX, (h + dh) % NH
            hid[dx, dh] = send(block(mine, ht), region(x, h, mine), device(xt, ht, yl, z, c))

    def weight_rows(xs, low, size):
        return pl.ds(pl.multiple_of(xs * width + low, TILE), size)

    def head_spot(kx, low, size):
        return heads.at[pl.ds(low, size), pl.ds(pl.multiple_of(kx * depth, depth), depth)]

    wgt = []

    def spread_weight():
        if len(wgt) < len(chunks):
            low, size = chunks[len(wgt)]
            wgt.append(
                [
                    send(
                        padded.at[weight_rows((x + dx) % NX, low, size), :],
                        head_spot(x, low, size),
                        device((x + dx) % NX, h, yl, z, c),
                    )
                    for dx in (1, 3, 2)
                ]
            )

    fwd, near_core, far_core, met = {}, {}, {}, {}

    def source(peer):
        return (x - peer[0] + NX) % NX, (h + peer[1]) % NH

    def pass_on(peers):
        for peer in peers:
            spot = region(*source(peer), mine)
            arrived(spot, hid[peer])
            fwd[peer] = send(spot, spot, device(x, h, yl, z_pair, c))
            near_core[peer] = send(spot, spot, mate)

    def pass_core(peers):
        for peer in peers:
            spot = region(*source(peer), other)
            arrived(spot, fwd[peer])
            far_core[peer] = send(spot, spot, mate)

    def collect(peers):
        for peer in peers:
            xs, hs = source(peer)
            arrived(region(xs, hs, 2 * (1 - c) + parity), near_core[peer])
            arrived(region(xs, hs, 2 * (1 - c) + 1 - parity), far_core[peer])

    spread(above)
    spread_weight()
    spread_weight()
    for dx, dh in GROUP_PEERS:
        met[dx, dh] = send(meta, metas.at[g], device((x + dx) % NX, (h + dh) % NH, yl, z, c))
    locals_ = [
        pltpu.make_async_copy(block(kx, h), region(x, h, kx), local_sem.at[kx]) for kx in range(NX)
    ]
    locals_.append(
        pltpu.make_async_copy(
            padded.at[weight_rows(x, 0, width), :], head_spot(x, 0, width), local_sem.at[NX]
        )
    )
    for copy in locals_:
        copy.start()

    loads[2].wait()
    teacher[...] = jnp.zeros_like(teacher)
    for side in range(NC):
        teacher[side, :, 0:slab] = panel_ref[:, side * slab : (side + 1) * slab]

    pass_on(above)
    spread_weight()
    pass_core(above)
    spread(beside)
    spread_weight()
    for copy in locals_:
        copy.wait()
    for peer in GROUP_PEERS:
        xs, hs = source(peer)
        arrived(metas.at[xs * 2 + hs], met[peer])
    collect(above)

    def product(side, low, size):
        return lax.dot_general(
            wide[pl.ds(pl.multiple_of(side * half, half), half), :],
            heads[low : low + size, :],
            (((1,), (1,)), ((), ())),
            preferred_element_type=jnp.float32,
        )

    def teach_spot(xs, cs):
        step = rows // 2
        return teach.at[pl.ds(pl.multiple_of(xs * rows + cs * step, step), step), :]

    def teacher_piece(xt, ct):
        return teacher.at[ct, :, pl.ds(pl.multiple_of(xt * width, TILE), width)]

    halves, teaching = [], []
    for j, (low, size) in enumerate(chunks):
        for k, dx in enumerate((1, 3, 2)):
            arrived(head_spot((x - dx + NX) % NX, low, size), wgt[j][k])
        partial[:, low : low + size] = product(1 - h, low, size)
        piece = pl.ds(low, size)
        halves.append(send(partial.at[:, piece], landed.at[:, piece], partner))
        spread_weight()
        if j == 1:
            pass_on(beside)
        if j == 2:
            pass_core(beside)
        if j == len(chunks) - 2:
            keep = pltpu.make_async_copy(teacher_piece(x, c), teach_spot(x, c), local_sem.at[0])
            keep.start()
            for dx, dc in PAIR_PEERS:
                xt, ct = (x + dx) % NX, (c + dc) % NC
                teaching.append(send(teacher_piece(xt, ct), teach_spot(x, c), device(xt, h, yl, z, ct)))
    collect(beside)
    for low in range(0, width, 256):
        size = min(256, width - low)
        logits[:, low : low + size] = product(h, low, size)

    step = rows // 2
    lane = lax.broadcasted_iota(jnp.int32, (step, TILE), 1)
    column = lax.broadcasted_iota(jnp.int32, (step, width), 1)
    inside = column < slab - x * width
    base = (v * slab + x * width).astype(jnp.float32)
    column_f = column.astype(jnp.float32)

    def fill(group, carry):
        cols[pl.ds(pl.multiple_of(group * rows, rows), rows), :] = to_columns(metas[group * 2 + h])
        return carry

    lax.fori_loop(0, NX, fill, 0)
    keep.wait()
    for k, (dx, dc) in enumerate(PAIR_PEERS):
        arrived(teach_spot((x - dx + NX) % NX, (c + dc) % NC), teaching[k])

    def measure_teacher(i, carry):
        span = pl.ds(pl.multiple_of(i * step, step), step)
        raw = teach[span, :].astype(jnp.float32)
        masked = jnp.where(inside, raw, LOW)
        old = cols[span, :]
        chosen = (column_f == old[:, 0:1] - base) & inside
        peak = jnp.max(masked, axis=1, keepdims=True)
        total = jnp.sum(jnp.exp(masked - peak), axis=1, keepdims=True)
        pick = jnp.sum(jnp.where(chosen, raw, 0.0), axis=1, keepdims=True)
        table = jnp.where(lane == 4, peak, jnp.where(lane == 5, total, pick))
        cols[span, :] = jnp.where(lane == 0, old, table)
        return carry

    lax.fori_loop(0, half // step, measure_teacher, 0)
    for j, (low, size) in enumerate(chunks):
        arrived(landed.at[:, pl.ds(low, size)], halves[j])

    def measure_student(i, carry):
        span = pl.ds(pl.multiple_of(i * step, step), step)
        student = jnp.where(inside, logits[span, :] + landed[span, :], LOW)
        logits[span, :] = student
        raw = teach[span, :].astype(jnp.float32)
        old = cols[span, :]
        chosen = (column_f == old[:, 0:1] - base) & inside
        peak = jnp.max(student, axis=1, keepdims=True)
        exps = jnp.exp(student - peak)
        found = {
            1: peak,
            2: jnp.sum(exps, axis=1, keepdims=True),
            3: jnp.sum(exps * (student - raw), axis=1, keepdims=True),
            6: jnp.sum(jnp.where(chosen, student, 0.0), axis=1, keepdims=True),
        }
        for k, value in found.items():
            old = jnp.where(lane == k, value, old)
        cols[span, :] = old
        return carry

    lax.fori_loop(0, half // step, measure_student, 0)

    def pack(group, carry):
        table = jnp.transpose(cols[pl.ds(pl.multiple_of(group * rows, rows), rows), :])
        near[0, group] = table[0:8]
        return carry

    lax.fori_loop(0, NX, pack, 0)
    slots = [
        send(near.at[0], near.at[k + 1], device((x + dx) % NX, h, yl, z, (c + dc) % NC))
        for k, (dx, dc) in enumerate(PAIR_PEERS)
    ]
    for k, slot in enumerate(slots):
        arrived(near.at[k + 1], slot)
    for k, value in enumerate(merge(near[:, :, 1:8])):
        merged[:, k] = value
    merged[:, 7] = near[0, :, 0]
    pair = pl.ds(2 * c, 2)
    slots = [
        send(merged.at[pair], far.at[k + 1], device(x, h, (yl + dy) % NYL, (z + dz) % NZ, c))
        for k, (dy, dz) in enumerate(LINE_PEERS)
    ]
    far[0] = merged[pair]
    for side in range(NH):
        for p in range(NX):
            start, spot = side * half + p * rows, p * 2 * rows + side * rows
            own[spot : spot + rows, :] = wide[
                start : start + rows, pl.ds(pl.multiple_of(x * depth, depth), depth)
            ]
    for k, slot in enumerate(slots):
        arrived(far.at[k + 1], slot)
    peak_s, sum_s, weighted, peak_t, sum_t, pick_s, pick_t = merge(far[...])

    total_rows = jnp.sum(metas[:, 1, 0:1])
    student_norm = peak_s + jnp.log(sum_s)
    teacher_norm = peak_t + jnp.log(sum_t)
    mean_gap = weighted / sum_s
    divergence = mean_gap - student_norm + teacher_norm
    advantage = (pick_t - teacher_norm) - (pick_s - student_norm)
    counts = jnp.stack([metas[(2 * c + k) * 2 + h][1] for k in range(2)], axis=0)
    valid = lax.broadcasted_iota(jnp.int32, (2, rows), 1).astype(jnp.float32) < counts
    row_weight = jnp.where(valid, rows / total_rows, 0.0)
    kl = jnp.where(valid, divergence, 0.0)
    token_row = far[0, :, 7]
    table = [
        peak_s, 1.0 / sum_s, mean_gap, row_weight * KL_SCALE, row_weight * advantage, token_row, kl, kl,
    ]
    for k, value in enumerate(table):
        outcome[pair, k] = value
    slot = send(outcome.at[pair], outcome.at[pair], mate)
    arrived(outcome.at[pl.ds(2 - 2 * c, 2)], slot)
    kl_ref[...] = outcome[x, 6:7]

    def place_of(xs, hs, p, low=0, size=None):
        start = pl.multiple_of(p * 2 * rows + hs * rows + low, step)
        return every.at[xs, pl.ds(start, rows if size is None else size), :]

    per = rows // step

    def finish(i, carry):
        span = pl.ds(pl.multiple_of(i * step, step), step)
        goal = pl.ds(pl.multiple_of((i // per * 2 + h) * rows + i % per * step, step), step)
        student = logits[span, :]
        raw = teach[span, :].astype(jnp.float32)
        table = cols[span, :]
        probs = jnp.exp(student - table[:, 0:1]) * table[:, 1:2]
        chosen = (column_f == table[:, 5:6] - base) & inside
        adv = table[:, 4:5]
        grad = probs * (table[:, 3:4] * ((student - raw) - table[:, 2:3]) + adv)
        grad = grad - jnp.where(chosen, adv, 0.0)
        every[x, goal, :] = grad.astype(jnp.bfloat16)
        return carry

    direct = []

    def spread_grad():
        if len(direct) < NX:
            spot = place_of(x, h, len(direct))
            direct.append([send(spot, spot, to_right), send(spot, spot, to_left), send(spot, spot, partner)])

    for p in range(NX):
        cols[p * rows : (p + 1) * rows, :] = to_columns(outcome[p])
        lax.fori_loop(p * per, (p + 1) * per, finish, 0)
        if p < 2:
            spread_grad()

    def rows_part(p):
        start = p * 2 * rows
        out = jnp.zeros((2 * rows, depth), jnp.float32)
        for xs in range(NX):
            out = out + jnp.dot(
                every[xs, start : start + 2 * rows, :],
                padded[xs * width : (xs + 1) * width, :],
                preferred_element_type=jnp.float32,
            )
        for side in range(NH):
            for s in range(4):
                rows_out[p, s % 2, s // 2, side] = out[
                    side * rows : (side + 1) * rows, s * TILE : (s + 1) * TILE
                ]
        return send(rows_out.at[p, 1 - c], paired.at[p], mate)

    lines = []

    def line_up(p, slot):
        arrived(paired.at[p], slot)
        for zt in range(NZ):
            span = pl.ds(zt % 4 * part, part)
            for b in range(NYL):
                staged[p, zt, b] = rows_out[p, c, b, zt // 4, span, :] + paired[p, b, zt // 4, span, :]
        lines.append(
            [
                send(
                    staged.at[p, (z + dz) % NZ], lined.at[p, dz], device(x, h, yl, (z + dz) % NZ, c)
                )
                for dz in range(1, NZ)
            ]
        )

    def deliver(p):
        for dz in range(1, NZ):
            arrived(lined.at[p, dz], lines[p][dz - 1])
        total = staged[p, z]
        for dz in range(1, NZ):
            total = total + lined[p, dz]
        cross_out[p] = total
        span = pl.ds(pl.multiple_of(quarter * part, part), part)
        for b in range(NYL):

            @pl.when(leaves[p, b])
            def _():
                pltpu.make_async_remote_copy(
                    src_ref=cross_out.at[p, b], dst_ref=final_in.at[yl, span, :],
                    send_sem=end_sent.at[p * NYL + b], recv_sem=end_got.at[yl * 4 + quarter],
                    device_id={"grp": goals[p, b][0], "vocab": goals[p, b][1]}, device_id_type=MESH,
                ).start()

            @pl.when(jnp.logical_not(leaves[p, b]))
            def _():
                final_in[yl, span, :] = cross_out[p, b]

    far_own, last, paired_slots = [], [], []
    for p in range(NX + 3):
        if p < NX:
            arrived(place_of(left, h, p), direct[p][0])
            lead = place_of(left, h, p, 0, step)
            a = send(lead, lead, to_right)
            arrived(place_of(right, h, p), direct[p][1])
            tail = place_of(right, h, p, step, step)
            far_own.append((a, send(tail, tail, to_left)))
            if p == NX - 1:
                lower = place_of(left, h, p, step, step)
                cross = [send(lower, lower, partner), send(tail, tail, partner)]
            spread_grad()
        if 1 <= p <= NX:
            q = p - 1
            arrived(place_of(opposite, h, q, 0, step), far_own[q][0])
            arrived(place_of(opposite, h, q, step, step), far_own[q][1])
            spot = place_of(opposite, h, q)
            far_half = send(spot, spot, partner)
            spot = place_of(x, 1 - h, q)
            arrived(spot, direct[q][2])
            if q == NX - 1:
                spot = place_of(x, 1 - h, q, 0, step)
            last.append([send(spot, spot, to_right), send(spot, spot, to_left), far_half])
        if 3 <= p:
            line_up(p - 3, paired_slots[p - 3])
        if 2 <= p <= NX + 1:
            q = p - 2
            size = rows
            if q == NX - 1:
                size = step
                arrived(place_of(left, 1 - h, q, step, step), cross[0])
                arrived(place_of(right, 1 - h, q, step, step), cross[1])
            arrived(place_of(left, 1 - h, q, 0, size), last[q][0])
            arrived(place_of(right, 1 - h, q, 0, size), last[q][1])
            arrived(place_of(opposite, 1 - h, q), last[q][2])
            paired_slots.append(rows_part(q))
    for p in range(NX - 2):
        deliver(p)

    for xs in range(NX):
        out = lax.dot_general(
            every[xs], own[...], (((0,), (0,)), ((), ())), preferred_element_type=jnp.float32
        )
        head_ref[xs * width : (xs + 1) * width, :] = out.astype(jnp.bfloat16)
    store = pltpu.make_async_copy(head_ref, head_hbm, local_sem.at[NX + 2])
    store.start()
    for p in (NX - 2, NX - 1):
        deliver(p)
    for b, k in origins:

        @pl.when(comes[b, k])
        def _():
            spot = final_in.at[b, pl.ds(k * part, part), :]
            pltpu.make_async_copy(spot, spot, end_got.at[b * 4 + k]).wait()

    out_ref[...] = (final_in[0] + final_in[1]).astype(jnp.bfloat16)
    for p, b in goals:

        @pl.when(leaves[p, b])
        def _():
            spot = cross_out.at[p, b]
            pltpu.make_async_copy(spot, spot, end_sent.at[p * NYL + b]).wait()

    for copy in pending:
        copy.wait_send()
    store.wait()


def shards(hidden, weight, teacher_panels, token_ids, row_counts):
    rows = hidden.shape[0]
    depth, slab = weight.shape
    width = -(-slab // (NX * TILE)) * TILE
    half, tokens = NX * rows, NX * NH * rows
    chunks = tuple((low, TILE) for low in range(0, width, TILE))
    turned = weight.T
    whole = slab // 16 * 16
    tail = jnp.pad(turned[whole:], ((0, 16 - (slab - whole)), (0, 0)))
    m, q = len(PAIR_PEERS), len(LINE_PEERS)
    part = rows * NH // NZ
    vmem = pl.BlockSpec(memory_space=pltpu.VMEM)
    hbm = pl.BlockSpec(memory_space=pl.ANY)
    f32, bf16 = jnp.float32, jnp.bfloat16
    copies = 5 * len(GROUP_PEERS) + 4 * len(chunks) + 2 * m + q + (9 + NZ - 1) * NX + 3
    head_grad, hidden_grad, kl = pl.pallas_call(
        functools.partial(fused_kernel, slab, chunks),
        name="distill",
        out_shape=[
            jax.ShapeDtypeStruct((NX * width, depth), bf16),
            jax.ShapeDtypeStruct((rows, TILE), bf16),
            jax.ShapeDtypeStruct((1, rows), f32),
        ],
        in_specs=[hbm] * 3 + [vmem] * 2 + [pl.BlockSpec(memory_space=pltpu.SMEM)],
        out_specs=[hbm, vmem, vmem],
        scratch_shapes=[
            pltpu.VMEM(hidden.shape, bf16),
            pltpu.VMEM((NX * width, depth), bf16),
            pltpu.VMEM(teacher_panels.shape, bf16),
            pltpu.VMEM((NX * width, depth), bf16),
            pltpu.VMEM((tokens, NX * depth), bf16),
            pltpu.VMEM((width, NX * depth), bf16),
            pltpu.VMEM((half, width), f32),
            pltpu.VMEM((half, width), f32),
            pltpu.VMEM((half, width), f32),
            pltpu.VMEM((NC, rows // 2, NX * width), bf16),
            pltpu.VMEM((half, width), bf16),
            pltpu.VMEM((8, rows), f32),
            pltpu.VMEM((NX * NH, 8, rows), f32),
            pltpu.VMEM((m + 1, NX, 8, rows), f32),
            pltpu.VMEM((q + 1, 2, 8, rows), f32),
            pltpu.VMEM((NX, 8, rows), f32),
            pltpu.VMEM((NX, 8, rows), f32),
            pltpu.VMEM((half, TILE), f32),
            pltpu.VMEM((NX, tokens, width), bf16),
            pltpu.VMEM((tokens, depth), bf16),
            pltpu.VMEM((NX, NC, NYL, NH, rows, TILE), f32),
            pltpu.VMEM((NX, NYL, NH, rows, TILE), f32),
            pltpu.VMEM((NX, NZ, NYL, part, TILE), f32),
            pltpu.VMEM((NX, NZ, NYL, part, TILE), f32),
            pltpu.VMEM((NX, NYL, part, TILE), f32),
            pltpu.VMEM((NYL, rows, TILE), f32),
            pltpu.SemaphoreType.DMA((NX + 4,)),
            pltpu.SemaphoreType.DMA((copies,)),
            pltpu.SemaphoreType.DMA((copies,)),
            pltpu.SemaphoreType.DMA((NX * NYL,)),
            pltpu.SemaphoreType.DMA((NYL * 4,)),
        ],
        compiler_params=pltpu.CompilerParams(
            collective_id=1, has_side_effects=True, vmem_limit_bytes=56 * 2**20
        ),
    )(hidden, turned, teacher_panels, tail, token_ids[None], row_counts)
    return kl[0], hidden_grad, head_grad[:slab].T


def solution(mesh):
    return jax.shard_map(
        shards,
        mesh=mesh,
        in_specs=(P("grp", None), P("grp", "vocab"), P("grp", "vocab"), P("grp"), P("grp")),
        out_specs=(P("grp"), P("grp", "vocab"), P("grp", "vocab")),
        check_vma=False,
    )
```

```python
import functools

import jax
import jax.numpy as jnp
from jax import lax
from jax.experimental import pallas as pl
from jax.experimental.pallas import tpu as pltpu
from jax.sharding import PartitionSpec as P

KL_SCALE = 256.0
MESH = pl.DeviceIdType.MESH
LOW = -1e30
NX, NH, NYL, NZ, NC = 4, 2, 2, 8, 2
TILE = 128
GROUP_PEERS = [(dx, dh) for dh in (1, 0) for dx in (0, 1, 3, 2) if dx or dh]
PAIR_PEERS = [(dx, dc) for dc in (0, 1) for dx in (1, 3, 2, 0) if dx or dc]
LINE_PEERS = [(dy, dz) for dy in (0, 1) for dz in range(NZ) if dy or dz]


def place():
    g = lax.axis_index("grp")
    v = lax.axis_index("vocab")
    return g // 2, g % 2, v // 16, (v // 2) % 8, v % 2


def device(x, h, yl, z, c):
    return {"grp": x * 2 + h, "vocab": yl * 16 + z * 2 + c}


def to_columns(tile):
    return jnp.transpose(jnp.concatenate([tile] * (TILE // 8), axis=0))


def merge(buf):
    peak_s = jnp.max(buf[:, :, 0], axis=0)
    scale_s = jnp.exp(buf[:, :, 0] - peak_s[None])
    peak_t = jnp.max(buf[:, :, 3], axis=0)
    scale_t = jnp.exp(buf[:, :, 3] - peak_t[None])
    return [
        peak_s,
        jnp.sum(buf[:, :, 1] * scale_s, axis=0),
        jnp.sum(buf[:, :, 2] * scale_s, axis=0),
        peak_t,
        jnp.sum(buf[:, :, 4] * scale_t, axis=0),
        jnp.sum(buf[:, :, 5], axis=0),
        jnp.sum(buf[:, :, 6], axis=0),
    ]


def fused_kernel(
    slab,
    chunks,
    hidden_hbm,
    weight_hbm,
    panel_hbm,
    tail_ref,
    token_ref,
    count_ref,
    head_hbm,
    out_ref,
    kl_ref,
    hidden_ref,
    head_ref,
    panel_ref,
    padded,
    wide,
    heads,
    partial,
    landed,
    logits,
    teacher,
    teach,
    meta,
    metas,
    near,
    far,
    merged,
    outcome,
    cols,
    every,
    own,
    rows_out,
    paired,
    staged,
    lined,
    cross_out,
    final_in,
    local_sem,
    sent,
    got,
    end_sent,
    end_got,
):
    x, h, yl, z, c = place()
    rows, depth = hidden_ref.shape[0], padded.shape[1]
    above = GROUP_PEERS[:NX]
    beside = GROUP_PEERS[NX:]
    half = NX * rows
    width = padded.shape[0] // NX
    z_pair = z + 1 - 2 * lax.rem(z, 2)
    g = x * 2 + h
    v = yl * 16 + z * 2 + c
    part = rows * NH // NZ
    quarter = lax.rem(z, 4)
    goals = {(p, b): (2 * p + z // 4, 4 * g + 2 * b + c) for p in range(NX) for b in range(NYL)}
    origins = {
        (b, k): (v // 4, b * 16 + ((g % 2) * 4 + k) * 2 + v % 2) for b in range(NYL) for k in range(4)
    }
    leaves = {key: (a != g) | (b != v) for key, (a, b) in goals.items()}
    comes = {key: (a != g) | (b != v) for key, (a, b) in origins.items()}
    partner = device(x, 1 - h, yl, z, c)
    mate = device(x, h, yl, z, 1 - c)
    right, left = (x + 1) % NX, (x + NX - 1) % NX
    opposite = (x + 2) % NX
    to_right, to_left = device(right, h, yl, z, c), device(left, h, yl, z, c)

    whole = slab // 16 * 16
    loads = [
        pltpu.make_async_copy(hidden_hbm, hidden_ref, local_sem.at[NX + 1]),
        pltpu.make_async_copy(
            weight_hbm.at[pl.ds(0, whole)], padded.at[pl.ds(0, whole)], local_sem.at[NX + 2]
        ),
        pltpu.make_async_copy(panel_hbm, panel_ref, local_sem.at[NX + 3]),
    ]
    for load in loads:
        load.start()
    barrier = pltpu.get_barrier_semaphore()
    peers = [device((x + dx) % NX, (h + dh) % NH, yl, z, c) for dx, dh in GROUP_PEERS]
    peers += [device((x + dx) % NX, h, yl, z, 1 - c) for dx in range(NX)]
    peers += [device(x, h, (yl + dy) % NYL, (z + dz) % NZ, c) for dy, dz in LINE_PEERS]
    for peer in peers:
        pl.semaphore_signal(barrier, inc=1, device_id=peer, device_id_type=MESH)

    for key, (a, b) in origins.items():

        @pl.when(comes[key])
        def _():
            pl.semaphore_signal(
                barrier, inc=1, device_id={"grp": a, "vocab": b}, device_id_type=MESH
            )

    meta[...] = jnp.where(
        lax.broadcasted_iota(jnp.int32, meta.shape, 0) == 0,
        token_ref[...].astype(jnp.float32),
        count_ref[0].astype(jnp.float32),
    )
    metas[g] = meta[...]
    padded[whole : whole + 16, :] = tail_ref[...]
    padded[whole + 16 :, :] = jnp.zeros((NX * width - whole - 16, depth), padded.dtype)
    loads[0].wait()
    loads[1].wait()
    others = sum(jnp.where(leave, 1, 0) for leave in leaves.values())
    pl.semaphore_wait(barrier, len(peers) + others)

    pending = []

    def send(src, dst, target):
        slot = len(pending)
        copy = pltpu.make_async_remote_copy(
            src_ref=src, dst_ref=dst, send_sem=sent.at[slot], recv_sem=got.at[slot],
            device_id=target, device_id_type=MESH,
        )
        copy.start()
        pending.append(copy)
        return slot

    def arrived(ref, slot):
        pltpu.make_async_copy(ref, ref, got.at[slot]).wait()

    parity = lax.rem(z, 2)
    mine, other = 2 * c + parity, 2 * c + 1 - parity

    def region(xs, hs, kx):
        return wide.at[
            pl.ds(pl.multiple_of(hs * half + xs * rows, rows), rows),
            pl.ds(pl.multiple_of(kx * depth, depth), depth),
        ]

    def block(kx, hs):
        return hidden_ref.at[:, pl.ds(pl.multiple_of((kx * 2 + hs) * depth, depth), depth)]

    hid = {}

    def spread(peers):
        for dx, dh in peers:
            xt, ht = (x + dx) % NX, (h + dh) % NH
            hid[dx, dh] = send(block(mine, ht), region(x, h, mine), device(xt, ht, yl, z, c))

    def weight_rows(xs, low, size):
        return pl.ds(pl.multiple_of(xs * width + low, TILE), size)

    def head_spot(kx, low, size):
        return heads.at[pl.ds(low, size), pl.ds(pl.multiple_of(kx * depth, depth), depth)]

    wgt = []

    def spread_weight():
        if len(wgt) < len(chunks):
            low, size = chunks[len(wgt)]
            wgt.append(
                [
                    send(
                        padded.at[weight_rows((x + dx) % NX, low, size), :],
                        head_spot(x, low, size),
                        device((x + dx) % NX, h, yl, z, c),
                    )
                    for dx in (1, 3, 2)
                ]
            )

    fwd, near_core, far_core, met = {}, {}, {}, {}

    def source(peer):
        return (x - peer[0] + NX) % NX, (h + peer[1]) % NH

    def pass_on(peers):
        for peer in peers:
            spot = region(*source(peer), mine)
            arrived(spot, hid[peer])
            fwd[peer] = send(spot, spot, device(x, h, yl, z_pair, c))
            near_core[peer] = send(spot, spot, mate)

    def pass_core(peers):
        for peer in peers:
            spot = region(*source(peer), other)
            arrived(spot, fwd[peer])
            far_core[peer] = send(spot, spot, mate)

    def collect(peers):
        for peer in peers:
            xs, hs = source(peer)
            arrived(region(xs, hs, 2 * (1 - c) + parity), near_core[peer])
            arrived(region(xs, hs, 2 * (1 - c) + 1 - parity), far_core[peer])

    spread(above)
    spread_weight()
    spread_weight()
    spread_weight()
    for dx, dh in GROUP_PEERS:
        met[dx, dh] = send(meta, metas.at[g], device((x + dx) % NX, (h + dh) % NH, yl, z, c))
    locals_ = [
        pltpu.make_async_copy(block(kx, h), region(x, h, kx), local_sem.at[kx]) for kx in range(NX)
    ]
    locals_.append(
        pltpu.make_async_copy(
            padded.at[weight_rows(x, 0, width), :], head_spot(x, 0, width), local_sem.at[NX]
        )
    )
    for copy in locals_:
        copy.start()

    loads[2].wait()
    teacher[...] = jnp.zeros_like(teacher)
    for side in range(NC):
        teacher[side, :, 0:slab] = panel_ref[:, side * slab : (side + 1) * slab]

    pass_on(above)
    spread_weight()
    pass_core(above)
    spread(beside)
    spread_weight()
    for copy in locals_:
        copy.wait()
    for peer in GROUP_PEERS:
        xs, hs = source(peer)
        arrived(metas.at[xs * 2 + hs], met[peer])
    collect(above)

    def product(side, low, size):
        return lax.dot_general(
            wide[pl.ds(pl.multiple_of(side * half, half), half), :],
            heads[low : low + size, :],
            (((1,), (1,)), ((), ())),
            preferred_element_type=jnp.float32,
        )

    def teach_spot(xs, cs):
        step = rows // 2
        return teach.at[pl.ds(pl.multiple_of(xs * rows + cs * step, step), step), :]

    def teacher_piece(xt, ct):
        return teacher.at[ct, :, pl.ds(pl.multiple_of(xt * width, TILE), width)]

    halves, teaching = [], []
    for j, (low, size) in enumerate(chunks):
        for k, dx in enumerate((1, 3, 2)):
            arrived(head_spot((x - dx + NX) % NX, low, size), wgt[j][k])
        partial[:, low : low + size] = product(1 - h, low, size)
        piece = pl.ds(low, size)
        halves.append(send(partial.at[:, piece], landed.at[:, piece], partner))
        spread_weight()
        if j == 1:
            pass_on(beside)
        if j == 2:
            pass_core(beside)
        if j == len(chunks) - 2:
            keep = pltpu.make_async_copy(teacher_piece(x, c), teach_spot(x, c), local_sem.at[0])
            keep.start()
            for dx, dc in PAIR_PEERS:
                xt, ct = (x + dx) % NX, (c + dc) % NC
                teaching.append(send(teacher_piece(xt, ct), teach_spot(x, c), device(xt, h, yl, z, ct)))
    collect(beside)
    for low in range(0, width, 256):
        size = min(256, width - low)
        logits[:, low : low + size] = product(h, low, size)

    step = rows // 2
    lane = lax.broadcasted_iota(jnp.int32, (step, TILE), 1)
    column = lax.broadcasted_iota(jnp.int32, (step, width), 1)
    inside = column < slab - x * width
    base = (v * slab + x * width).astype(jnp.float32)
    column_f = column.astype(jnp.float32)

    def fill(group, carry):
        cols[pl.ds(pl.multiple_of(group * rows, rows), rows), :] = to_columns(metas[group * 2 + h])
        return carry

    lax.fori_loop(0, NX, fill, 0)
    keep.wait()
    for k, (dx, dc) in enumerate(PAIR_PEERS):
        arrived(teach_spot((x - dx + NX) % NX, (c + dc) % NC), teaching[k])

    def measure_teacher(i, carry):
        span = pl.ds(pl.multiple_of(i * step, step), step)
        raw = teach[span, :].astype(jnp.float32)
        masked = jnp.where(inside, raw, LOW)
        old = cols[span, :]
        chosen = (column_f == old[:, 0:1] - base) & inside
        peak = jnp.max(masked, axis=1, keepdims=True)
        total = jnp.sum(jnp.exp(masked - peak), axis=1, keepdims=True)
        pick = jnp.sum(jnp.where(chosen, raw, 0.0), axis=1, keepdims=True)
        table = jnp.where(lane == 4, peak, jnp.where(lane == 5, total, pick))
        cols[span, :] = jnp.where(lane == 0, old, table)
        return carry

    lax.fori_loop(0, half // step, measure_teacher, 0)
    for j, (low, size) in enumerate(chunks):
        arrived(landed.at[:, pl.ds(low, size)], halves[j])

    def measure_student(i, carry):
        span = pl.ds(pl.multiple_of(i * step, step), step)
        student = jnp.where(inside, logits[span, :] + landed[span, :], LOW)
        logits[span, :] = student
        raw = teach[span, :].astype(jnp.float32)
        old = cols[span, :]
        chosen = (column_f == old[:, 0:1] - base) & inside
        peak = jnp.max(student, axis=1, keepdims=True)
        exps = jnp.exp(student - peak)
        found = {
            1: peak,
            2: jnp.sum(exps, axis=1, keepdims=True),
            3: jnp.sum(exps * (student - raw), axis=1, keepdims=True),
            6: jnp.sum(jnp.where(chosen, student, 0.0), axis=1, keepdims=True),
        }
        for k, value in found.items():
            old = jnp.where(lane == k, value, old)
        cols[span, :] = old
        return carry

    lax.fori_loop(0, half // step, measure_student, 0)

    def pack(group, carry):
        table = jnp.transpose(cols[pl.ds(pl.multiple_of(group * rows, rows), rows), :])
        near[0, group] = table[0:8]
        return carry

    lax.fori_loop(0, NX, pack, 0)
    slots = [
        send(near.at[0], near.at[k + 1], device((x + dx) % NX, h, yl, z, (c + dc) % NC))
        for k, (dx, dc) in enumerate(PAIR_PEERS)
    ]
    for k, slot in enumerate(slots):
        arrived(near.at[k + 1], slot)
    for k, value in enumerate(merge(near[:, :, 1:8])):
        merged[:, k] = value
    merged[:, 7] = near[0, :, 0]
    pair = pl.ds(2 * c, 2)
    slots = [
        send(merged.at[pair], far.at[k + 1], device(x, h, (yl + dy) % NYL, (z + dz) % NZ, c))
        for k, (dy, dz) in enumerate(LINE_PEERS)
    ]
    far[0] = merged[pair]
    for side in range(NH):
        for p in range(NX):
            start, spot = side * half + p * rows, p * 2 * rows + side * rows
            own[spot : spot + rows, :] = wide[
                start : start + rows, pl.ds(pl.multiple_of(x * depth, depth), depth)
            ]
    for k, slot in enumerate(slots):
        arrived(far.at[k + 1], slot)
    peak_s, sum_s, weighted, peak_t, sum_t, pick_s, pick_t = merge(far[...])

    total_rows = jnp.sum(metas[:, 1, 0:1])
    student_norm = peak_s + jnp.log(sum_s)
    teacher_norm = peak_t + jnp.log(sum_t)
    mean_gap = weighted / sum_s
    divergence = mean_gap - student_norm + teacher_norm
    advantage = (pick_t - teacher_norm) - (pick_s - student_norm)
    counts = jnp.stack([metas[(2 * c + k) * 2 + h][1] for k in range(2)], axis=0)
    valid = lax.broadcasted_iota(jnp.int32, (2, rows), 1).astype(jnp.float32) < counts
    row_weight = jnp.where(valid, rows / total_rows, 0.0)
    kl = jnp.where(valid, divergence, 0.0)
    token_row = far[0, :, 7]
    table = [
        peak_s, 1.0 / sum_s, mean_gap, row_weight * KL_SCALE, row_weight * advantage, token_row, kl, kl,
    ]
    for k, value in enumerate(table):
        outcome[pair, k] = value
    slot = send(outcome.at[pair], outcome.at[pair], mate)
    arrived(outcome.at[pl.ds(2 - 2 * c, 2)], slot)
    kl_ref[...] = outcome[x, 6:7]

    def place_of(xs, hs, p, low=0, size=None):
        start = pl.multiple_of(p * 2 * rows + hs * rows + low, step)
        return every.at[xs, pl.ds(start, rows if size is None else size), :]

    per = rows // step

    def finish(i, carry):
        span = pl.ds(pl.multiple_of(i * step, step), step)
        goal = pl.ds(pl.multiple_of((i // per * 2 + h) * rows + i % per * step, step), step)
        student = logits[span, :]
        raw = teach[span, :].astype(jnp.float32)
        table = cols[span, :]
        probs = jnp.exp(student - table[:, 0:1]) * table[:, 1:2]
        chosen = (column_f == table[:, 5:6] - base) & inside
        adv = table[:, 4:5]
        grad = probs * (table[:, 3:4] * ((student - raw) - table[:, 2:3]) + adv)
        grad = grad - jnp.where(chosen, adv, 0.0)
        every[x, goal, :] = grad.astype(jnp.bfloat16)
        return carry

    direct = []

    def spread_grad():
        if len(direct) < NX:
            spot = place_of(x, h, len(direct))
            direct.append([send(spot, spot, to_right), send(spot, spot, to_left), send(spot, spot, partner)])

    for p in range(NX):
        cols[p * rows : (p + 1) * rows, :] = to_columns(outcome[p])
        lax.fori_loop(p * per, (p + 1) * per, finish, 0)
        if p < 2:
            spread_grad()

    def rows_part(p):
        start = p * 2 * rows
        out = jnp.zeros((2 * rows, depth), jnp.float32)
        for xs in range(NX):
            out = out + jnp.dot(
                every[xs, start : start + 2 * rows, :],
                padded[xs * width : (xs + 1) * width, :],
                preferred_element_type=jnp.float32,
            )
        for side in range(NH):
            for s in range(4):
                rows_out[p, s % 2, s // 2, side] = out[
                    side * rows : (side + 1) * rows, s * TILE : (s + 1) * TILE
                ]
        return send(rows_out.at[p, 1 - c], paired.at[p], mate)

    lines = []

    def line_up(p, slot):
        arrived(paired.at[p], slot)
        for zt in range(NZ):
            span = pl.ds(zt % 4 * part, part)
            for b in range(NYL):
                staged[p, zt, b] = rows_out[p, c, b, zt // 4, span, :] + paired[p, b, zt // 4, span, :]
        lines.append(
            [
                send(
                    staged.at[p, (z + dz) % NZ], lined.at[p, dz], device(x, h, yl, (z + dz) % NZ, c)
                )
                for dz in range(1, NZ)
            ]
        )

    def deliver(p):
        for dz in range(1, NZ):
            arrived(lined.at[p, dz], lines[p][dz - 1])
        total = staged[p, z]
        for dz in range(1, NZ):
            total = total + lined[p, dz]
        cross_out[p] = total
        span = pl.ds(pl.multiple_of(quarter * part, part), part)
        for b in range(NYL):

            @pl.when(leaves[p, b])
            def _():
                pltpu.make_async_remote_copy(
                    src_ref=cross_out.at[p, b], dst_ref=final_in.at[yl, span, :],
                    send_sem=end_sent.at[p * NYL + b], recv_sem=end_got.at[yl * 4 + quarter],
                    device_id={"grp": goals[p, b][0], "vocab": goals[p, b][1]}, device_id_type=MESH,
                ).start()

            @pl.when(jnp.logical_not(leaves[p, b]))
            def _():
                final_in[yl, span, :] = cross_out[p, b]

    far_own, last, paired_slots = [], [], []
    for p in range(NX + 3):
        if p < NX:
            arrived(place_of(left, h, p), direct[p][0])
            lead = place_of(left, h, p, 0, step)
            a = send(lead, lead, to_right)
            arrived(place_of(right, h, p), direct[p][1])
            tail = place_of(right, h, p, step, step)
            far_own.append((a, send(tail, tail, to_left)))
            if p == NX - 1:
                lower = place_of(left, h, p, step, step)
                cross = [send(lower, lower, partner), send(tail, tail, partner)]
            spread_grad()
        if 1 <= p <= NX:
            q = p - 1
            arrived(place_of(opposite, h, q, 0, step), far_own[q][0])
            arrived(place_of(opposite, h, q, step, step), far_own[q][1])
            spot = place_of(opposite, h, q)
            far_half = send(spot, spot, partner)
            spot = place_of(x, 1 - h, q)
            arrived(spot, direct[q][2])
            if q == NX - 1:
                spot = place_of(x, 1 - h, q, 0, step)
            last.append([send(spot, spot, to_right), send(spot, spot, to_left), far_half])
        if 3 <= p:
            line_up(p - 3, paired_slots[p - 3])
        if 2 <= p <= NX + 1:
            q = p - 2
            size = rows
            if q == NX - 1:
                size = step
                arrived(place_of(left, 1 - h, q, step, step), cross[0])
                arrived(place_of(right, 1 - h, q, step, step), cross[1])
            arrived(place_of(left, 1 - h, q, 0, size), last[q][0])
            arrived(place_of(right, 1 - h, q, 0, size), last[q][1])
            arrived(place_of(opposite, 1 - h, q), last[q][2])
            paired_slots.append(rows_part(q))
    for p in range(NX - 2):
        deliver(p)

    for xs in range(NX):
        out = lax.dot_general(
            every[xs], own[...], (((0,), (0,)), ((), ())), preferred_element_type=jnp.float32
        )
        head_ref[xs * width : (xs + 1) * width, :] = out.astype(jnp.bfloat16)
    store = pltpu.make_async_copy(head_ref, head_hbm, local_sem.at[NX + 2])
    store.start()
    for p in (NX - 2, NX - 1):
        deliver(p)
    for b, k in origins:

        @pl.when(comes[b, k])
        def _():
            spot = final_in.at[b, pl.ds(k * part, part), :]
            pltpu.make_async_copy(spot, spot, end_got.at[b * 4 + k]).wait()

    out_ref[...] = (final_in[0] + final_in[1]).astype(jnp.bfloat16)
    for p, b in goals:

        @pl.when(leaves[p, b])
        def _():
            spot = cross_out.at[p, b]
            pltpu.make_async_copy(spot, spot, end_sent.at[p * NYL + b]).wait()

    for copy in pending:
        copy.wait_send()
    store.wait()


def shards(hidden, weight, teacher_panels, token_ids, row_counts):
    rows = hidden.shape[0]
    depth, slab = weight.shape
    width = -(-slab // (NX * TILE)) * TILE
    half, tokens = NX * rows, NX * NH * rows
    chunks = tuple((low, TILE) for low in range(0, width, TILE))
    turned = weight.T
    whole = slab // 16 * 16
    tail = jnp.pad(turned[whole:], ((0, 16 - (slab - whole)), (0, 0)))
    m, q = len(PAIR_PEERS), len(LINE_PEERS)
    part = rows * NH // NZ
    vmem = pl.BlockSpec(memory_space=pltpu.VMEM)
    hbm = pl.BlockSpec(memory_space=pl.ANY)
    f32, bf16 = jnp.float32, jnp.bfloat16
    copies = 5 * len(GROUP_PEERS) + 4 * len(chunks) + 2 * m + q + (9 + NZ - 1) * NX + 3
    head_grad, hidden_grad, kl = pl.pallas_call(
        functools.partial(fused_kernel, slab, chunks),
        name="distill",
        out_shape=[
            jax.ShapeDtypeStruct((NX * width, depth), bf16),
            jax.ShapeDtypeStruct((rows, TILE), bf16),
            jax.ShapeDtypeStruct((1, rows), f32),
        ],
        in_specs=[hbm] * 3 + [vmem] * 2 + [pl.BlockSpec(memory_space=pltpu.SMEM)],
        out_specs=[hbm, vmem, vmem],
        scratch_shapes=[
            pltpu.VMEM(hidden.shape, bf16),
            pltpu.VMEM((NX * width, depth), bf16),
            pltpu.VMEM(teacher_panels.shape, bf16),
            pltpu.VMEM((NX * width, depth), bf16),
            pltpu.VMEM((tokens, NX * depth), bf16),
            pltpu.VMEM((width, NX * depth), bf16),
            pltpu.VMEM((half, width), f32),
            pltpu.VMEM((half, width), f32),
            pltpu.VMEM((half, width), f32),
            pltpu.VMEM((NC, rows // 2, NX * width), bf16),
            pltpu.VMEM((half, width), bf16),
            pltpu.VMEM((8, rows), f32),
            pltpu.VMEM((NX * NH, 8, rows), f32),
            pltpu.VMEM((m + 1, NX, 8, rows), f32),
            pltpu.VMEM((q + 1, 2, 8, rows), f32),
            pltpu.VMEM((NX, 8, rows), f32),
            pltpu.VMEM((NX, 8, rows), f32),
            pltpu.VMEM((half, TILE), f32),
            pltpu.VMEM((NX, tokens, width), bf16),
            pltpu.VMEM((tokens, depth), bf16),
            pltpu.VMEM((NX, NC, NYL, NH, rows, TILE), f32),
            pltpu.VMEM((NX, NYL, NH, rows, TILE), f32),
            pltpu.VMEM((NX, NZ, NYL, part, TILE), f32),
            pltpu.VMEM((NX, NZ, NYL, part, TILE), f32),
            pltpu.VMEM((NX, NYL, part, TILE), f32),
            pltpu.VMEM((NYL, rows, TILE), f32),
            pltpu.SemaphoreType.DMA((NX + 4,)),
            pltpu.SemaphoreType.DMA((copies,)),
            pltpu.SemaphoreType.DMA((copies,)),
            pltpu.SemaphoreType.DMA((NX * NYL,)),
            pltpu.SemaphoreType.DMA((NYL * 4,)),
        ],
        compiler_params=pltpu.CompilerParams(
            collective_id=1, has_side_effects=True, vmem_limit_bytes=56 * 2**20
        ),
    )(hidden, turned, teacher_panels, tail, token_ids[None], row_counts)
    return kl[0], hidden_grad, head_grad[:slab].T


def solution(mesh):
    return jax.shard_map(
        shards,
        mesh=mesh,
        in_specs=(P("grp", None), P("grp", "vocab"), P("grp", "vocab"), P("grp"), P("grp")),
        out_specs=(P("grp"), P("grp", "vocab"), P("grp", "vocab")),
        check_vma=False,
    )
```
